32 devices in a mesh: grp: 2 (over x), row: 16 (over z, y, core).
Axes of the slice: x: 2, y: 2, z: 4, core: 2. Of those that a mesh axis runs over, the one named last changes fastest.
Arguments:
- fields: bfloat16 [128, 128, 1024], P(('grp', 'row')), parts along dimension 0, may hold values from -6 to 6
- kernel: bfloat16 [7, 7, 2048], P(None, None, 'grp'), parts along dimension 2, may hold values from -0.875 to 0.875
- norm_gain: float32 [2048], P('grp'), parts along dimension 0, may hold values from 0.4 to 1.6
- proj_in: bfloat16 [2048, 4096], P(('grp', 'row')), parts along dimension 0, may hold values from -0.1875 to 0.1875
- proj_out: bfloat16 [8192, 1024], P('grp', 'row'), parts along dimension 0, may hold values from -0.09375 to 0.09375
- cotangent: bfloat16 [128, 128, 1024], P(('grp', 'row')), parts along dimension 0, may hold values from -6 to 6
Outputs:
- result: bfloat16 [128, 128, 1024], P(('grp', 'row')), parts along dimension 0
- fields_grad: bfloat16 [128, 128, 1024], P(('grp', 'row')), parts along dimension 0
- proj_in_grad: bfloat16 [2048, 4096], P(('grp', 'row')), parts along dimension 0
- proj_out_grad: bfloat16 [8192, 1024], P('grp', 'row'), parts along dimension 0
- kernel_grad: float32 [7, 7, 2048], P(None, None, 'grp'), parts along dimension 2
- gain_grad: float32 [2048], P('grp'), parts along dimension 0
The draws below stay inside these ranges and needn't reach their ends.
There are 2 independent parts, one for each index of `grp`. The reference program is written for one: setup_inputs(seed, part) draws one part's arguments, and reference() takes and returns one part's arrays. A program takes and returns all parts, laid end to end along the dimension named above; each array names one. Nothing has to cross between parts.
All inputs are finite; a program needn't handle non-finite values.
Results may differ from the reference program's by a relative error of at most 0.017.
Values may be sent and summed in bfloat16 or wider, within the bound.
No kernel may reach another device: no remote copies, remote signals or barrier semaphores. Data moves between devices by JAX's collectives and lax.ppermute only.
A program may use at most 128 MiB of HBM per device.

```python
import math
import jax
import jax.numpy as jnp
from jax import lax

CH = 1024
HID = 4096
KS = 7
LON = 128
LAT = 64
TOKENS = 8192
N_ROW = 16


def raised(array, rng, source, target, blocks, factor):
    def block_of(position):
        return (jnp.arange(array.shape[position]) // (array.shape[position] // blocks)).reshape((-1,) + (1,) * (array.ndim - 1 - position))

    first = jax.random.permutation(rng, blocks)[block_of(target)]
    far = (block_of(target) + blocks // 2) % blocks
    return jnp.where((block_of(source) == first) | (block_of(source) == far), factor * array, array)


def block_levels(own_key, dims, cuts, low, largest):
    def one(axis_at, parts):
        steps = jax.random.uniform(jax.random.fold_in(jax.random.fold_in(own_key, 6), axis_at), (parts,), jnp.float32, low / len(cuts), largest / len(cuts))
        return jnp.repeat(jnp.exp(steps), dims[axis_at] // parts).reshape((-1,) + (1,) * (len(dims) - axis_at - 1))

    gain = one(*cuts[0])
    for cut in cuts[1:]:
        gain = gain * one(*cut)
    return gain


def scatter_about(rng, shape, spread, limit, split=(), dtype=jnp.bfloat16):
    array = spread * jax.random.normal(rng, shape, jnp.float32)
    if split:
        array = array * block_levels(rng, shape, split, -0.22, 0.18)
    return jnp.clip(array, -limit, limit).astype(dtype)


def bell_draw_with(stream_key, shape, scale, limit, split, heavy, held_as=jnp.bfloat16):
    entries = scale * jax.random.normal(stream_key, shape, jnp.float32)
    if split:
        entries = entries * block_levels(stream_key, shape, split, -0.22, 0.18)
    return jnp.clip(raised(entries, jax.random.fold_in(stream_key, 3), *heavy), -limit, limit).astype(held_as)


def setup_inputs(seed: int = 0, part: int = 0) -> dict:
    key_of = jax.random.split(jax.random.key(seed), 7)
    part_splits = jax.random.split(jax.random.fold_in(key_of[6], part), 7)
    return {
        "fields": scatter_about(part_splits[0], (LAT, LON, CH), 1.0, 6.0, ((0, 16),)),
        "kernel": scatter_about(part_splits[1], (KS, KS, CH), (KS * KS) ** -0.5, 0.875),
        "norm_gain": jnp.clip(1.0 + 0.12 * jax.random.normal(part_splits[2], (CH,), jnp.float32), 0.4, 1.6),
        "proj_in": scatter_about(part_splits[3], (CH, HID), CH ** -0.5, 0.1875, ((0, 16),)),
        "proj_out": scatter_about(part_splits[4], (HID, CH), HID ** -0.5, 0.09375, ((1, 16),)),
        "cotangent": bell_draw_with(part_splits[5], (LAT, LON, CH), 1.0, 6.0, ((0, 16),), (0, 2, 16, 2.0)),
    }


def pad_grid(values):
    wrapped = jnp.concatenate([values[:, -3:], values, values[:, :3]], axis=1)
    return jnp.pad(wrapped, ((3, 3), (0, 0), (0, 0)))

def depthwise(padded, kernel):
    outcome = lax.conv_general_dilated(padded[None], kernel[:, :, None, :], (1, 1), 'VALID', dimension_numbers=('NHWC', 'HWIO', 'NHWC'), feature_group_count=kernel.shape[2], preferred_element_type=jnp.float32)
    return outcome[0]

def kernel_sums(conv_grad, padded):
    lat_rows = conv_grad.shape[0]
    lon_cells = conv_grad.shape[1]
    grad_wide = conv_grad.astype(jnp.float32)
    stacked = []
    for lat_off in range(KS):
        line = []
        for lon_off in range(KS):
            window = padded[lat_off:lat_off + lat_rows, lon_off:lon_off + lon_cells].astype(jnp.float32)
            line.append(lax.optimization_barrier(jnp.sum(grad_wide * window, axis=(0, 1))))
        stacked.append(jnp.stack(line))
    return jnp.stack(stacked)

def block_sum(left_side, right_side, grad_scale):
    left_blocks = left_side.reshape(N_ROW, -1, left_side.shape[1])
    right_blocks = right_side.reshape(N_ROW, -1, right_side.shape[1])

    def add_block(running, pair):
        device_term = jnp.dot(pair[0].T, pair[1], preferred_element_type=jnp.float32) * grad_scale
        rounded = lax.optimization_barrier(device_term.astype(jnp.bfloat16))
        return (running + rounded.astype(jnp.float32), None)
    start_sum = jnp.zeros((left_side.shape[1], right_side.shape[1]), jnp.float32)
    running, unused = lax.scan(add_block, start_sum, (left_blocks, right_blocks))
    return running.astype(jnp.bfloat16)

def reference(fields, kernel, norm_gain, proj_in, proj_out, cotangent):
    grad_scale = 1.0 / math.sqrt(TOKENS)
    padded = pad_grid(fields)
    conv_out = depthwise(padded, kernel)
    row_mean = lax.optimization_barrier(jnp.mean(conv_out, axis=-1, keepdims=True))
    centred = conv_out - row_mean
    inv_std = lax.rsqrt(lax.optimization_barrier(jnp.mean(centred * centred, axis=-1, keepdims=True)) + 1e-06)
    whitened = centred * inv_std
    normed = (whitened * norm_gain).astype(jnp.bfloat16)
    flat_norm = normed.reshape(-1, CH)
    pre_act = jnp.dot(flat_norm, proj_in, preferred_element_type=jnp.float32)
    gauss_area = 0.5 * (1.0 + jax.scipy.special.erf(pre_act / math.sqrt(2.0)))
    gauss_dens = jnp.exp(-0.5 * pre_act * pre_act) / math.sqrt(2.0 * math.pi)
    hidden = (pre_act * gauss_area).astype(jnp.bfloat16)
    branch = jnp.dot(hidden, proj_out, preferred_element_type=jnp.float32).reshape(fields.shape)
    result = (fields.astype(jnp.float32) + branch).astype(jnp.bfloat16)
    out_grad = cotangent.reshape(-1, CH)
    proj_out_grad = block_sum(hidden, out_grad, grad_scale)
    hidden_grad = jnp.dot(out_grad, proj_out.T, preferred_element_type=jnp.float32)
    pre_grad = (hidden_grad * (gauss_area + pre_act * gauss_dens)).astype(jnp.bfloat16)
    proj_in_grad = block_sum(flat_norm, pre_grad, grad_scale)
    norm_grad = jnp.dot(pre_grad, proj_in.T, preferred_element_type=jnp.float32).reshape(fields.shape)
    gain_grad = lax.optimization_barrier(jnp.sum(norm_grad * whitened, axis=(0, 1))) * grad_scale
    white_grad = norm_grad * norm_gain
    conv_grad = inv_std * (white_grad - lax.optimization_barrier(jnp.mean(white_grad, axis=-1, keepdims=True)) - whitened * lax.optimization_barrier(jnp.mean(white_grad * whitened, axis=-1, keepdims=True)))
    conv_grad = conv_grad.astype(jnp.bfloat16)
    kernel_grad = kernel_sums(conv_grad, padded) * grad_scale
    back_conv = depthwise(pad_grid(conv_grad), kernel[::-1, ::-1])
    fields_grad = (cotangent.astype(jnp.float32) + back_conv).astype(jnp.bfloat16)
    return (result, fields_grad, proj_in_grad, proj_out_grad, kernel_grad, gain_grad)
```

```python
import functools
import math

import jax
import jax.numpy as jnp
from jax import lax
from jax.experimental import pallas as pl
from jax.experimental.pallas import tpu as pltpu
from jax.sharding import PartitionSpec as P

F32 = jnp.float32
BF16 = jnp.bfloat16
KS = 7
RIM = KS // 2
LANES = 128
SUB = 8
MIB = 1024 * 1024


def cost(micros, nbytes=0):
    return pl.CostEstimate(flops=int(micros * 1.15e9), bytes_accessed=int(nbytes), transcendentals=0)


def params(mib):
    return pltpu.CompilerParams(vmem_limit_bytes=mib * MIB)


def whole(shape):
    return pl.BlockSpec(shape, lambda *_: (0,) * len(shape))


def fill_padded(before_ref, mid_ref, after_ref, pad_ref):
    lat, lon = mid_ref.shape[0], mid_ref.shape[1]
    for row in range(lat + 2 * RIM):
        if row < RIM:
            line = before_ref[row]
        elif row < RIM + lat:
            line = mid_ref[row - RIM]
        else:
            line = after_ref[row - RIM - lat]
        line = line.astype(F32)
        pad_ref[row, pl.ds(SUB, lon), :] = line
        pad_ref[row, pl.ds(0, SUB), :] = line[lon - SUB :]
        pad_ref[row, pl.ds(SUB + lon, SUB), :] = line[:SUB]


def conv_tile(pad_ref, weight_ref, start, lat, flip):
    totals = [None] * lat
    for b in range(KS):
        lines = [
            pad_ref[row, pl.ds(start + (SUB - RIM) + b, SUB), :] for row in range(lat + 2 * RIM)
        ]
        for a in range(KS):
            index = a * KS + b
            weight = weight_ref[KS * KS - 1 - index if flip else index]
            for row in range(lat):
                term = lines[row + a] * weight
                totals[row] = term if totals[row] is None else totals[row] + term
    return totals


def spread_weights(kern_ref, weight_ref):
    taps = kern_ref[...].astype(F32)
    for a in range(KS):
        for b in range(KS):
            weight_ref[a * KS + b] = jnp.broadcast_to(taps[a, b : b + 1], (SUB, LANES))


def forward_body(
    before_ref, mid_ref, after_ref, kern_ref, gain_ref, normed_ref, white_ref, inv_ref, pad_ref, weight_ref, conv_ref
):
    step = pl.program_id(0)
    lat, lon = mid_ref.shape[0], mid_ref.shape[1]
    blocks = conv_ref.shape[0]
    fill_padded(before_ref, mid_ref, after_ref, pad_ref)
    spread_weights(kern_ref, weight_ref)

    def tile(t, carry):
        start = pl.multiple_of(t * SUB, SUB)
        for row, total in enumerate(conv_tile(pad_ref, weight_ref, start, lat, False)):
            conv_ref[step, pl.ds(pl.multiple_of(row * lon + start, SUB), SUB), :] = total
        return carry

    lax.fori_loop(0, lon // SUB, tile, 0)

    @pl.when(step == blocks - 1)
    def _():
        channels = blocks * LANES
        high = 32

        def norm(t, carry):
            at = pl.ds(pl.multiple_of(t * high, high), high)
            parts = [conv_ref[j, at, :] for j in range(blocks)]
            mean = jnp.sum(functools.reduce(jnp.add, parts), axis=-1, keepdims=True) * (1.0 / channels)
            parts = [p - mean for p in parts]
            squares = functools.reduce(jnp.add, [p * p for p in parts])
            var = jnp.sum(squares, axis=-1, keepdims=True) * (1.0 / channels)
            inv = lax.rsqrt(var + 1e-06)
            inv_ref[at, :] = jnp.broadcast_to(inv, (high, LANES))
            for j in range(blocks):
                cols = slice(j * LANES, (j + 1) * LANES)
                white = parts[j] * inv
                white_ref[at, cols] = white
                normed_ref[at, cols] = (white * gain_ref[:, cols]).astype(BF16)
            return carry

        lax.fori_loop(0, conv_ref.shape[1] // high, norm, 0)


def forward_norm(before, mid, after, kernel, gain):
    lat, lon, channels = mid.shape
    tokens = lat * lon
    blocks = channels // LANES
    rows = lambda n: pl.BlockSpec((n, lon, LANES), lambda i: (0, 0, i))
    return pl.pallas_call(
        forward_body,
        grid=(blocks,),
        in_specs=[
            rows(RIM),
            rows(lat),
            rows(RIM),
            pl.BlockSpec((KS, KS, LANES), lambda i: (0, 0, i)),
            whole((1, channels)),
        ],
        out_specs=[whole((tokens, channels)), whole((tokens, channels)), whole((tokens, LANES))],
        out_shape=[
            jax.ShapeDtypeStruct((tokens, channels), BF16),
            jax.ShapeDtypeStruct((tokens, channels), F32),
            jax.ShapeDtypeStruct((tokens, LANES), F32),
        ],
        scratch_shapes=[
            pltpu.VMEM((lat + 2 * RIM, lon + 2 * SUB, LANES), F32),
            pltpu.VMEM((KS * KS, SUB, LANES), F32),
            pltpu.VMEM((blocks, tokens, LANES), F32),
        ],
        compiler_params=params(20),
        cost_estimate=cost(16),
        name="forward_norm",
    )(before, mid, after, kernel, gain.reshape(1, channels))


def backward_body(before_ref, mid_ref, after_ref, kern_ref, cot_ref, out_ref, pad_ref, weight_ref, sum_ref):
    lat, lon = mid_ref.shape[0], mid_ref.shape[1]
    fill_padded(before_ref, mid_ref, after_ref, pad_ref)
    spread_weights(kern_ref, weight_ref)

    def tile(t, carry):
        start = pl.multiple_of(t * SUB, SUB)
        for row, total in enumerate(conv_tile(pad_ref, weight_ref, start, lat, True)):
            sum_ref[row, pl.ds(start, SUB), :] = total
        return carry

    lax.fori_loop(0, lon // SUB, tile, 0)
    for row in range(lat):
        out_ref[row] = (cot_ref[row].astype(F32) + sum_ref[row]).astype(BF16)


def backward_conv(before, mid, after, kernel, cot):
    lat, lon, channels = mid.shape
    tokens = lat * lon
    rows = lambda n: pl.BlockSpec((n, lon, LANES), lambda i: (0, 0, i))
    return pl.pallas_call(
        backward_body,
        grid=(channels // LANES,),
        in_specs=[
            rows(RIM),
            rows(lat),
            rows(RIM),
            pl.BlockSpec((KS, KS, LANES), lambda i: (0, 0, i)),
            rows(lat),
        ],
        out_specs=rows(lat),
        out_shape=jax.ShapeDtypeStruct((lat, lon, channels), BF16),
        scratch_shapes=[
            pltpu.VMEM((lat + 2 * RIM, lon + 2 * SUB, LANES), F32),
            pltpu.VMEM((KS * KS, SUB, LANES), F32),
            pltpu.VMEM((lat, lon, LANES), F32),
        ],
        compiler_params=params(20),
        cost_estimate=cost(14),
        name="backward_conv",
    )(before, mid, after, kernel, cot)


def tap_sums_body(scale, before_ref, mid_ref, after_ref, grad_ref, out_ref, pad_ref, wide_ref):
    lat, lon = mid_ref.shape[0], mid_ref.shape[1]
    fill_padded(before_ref, mid_ref, after_ref, pad_ref)
    for row in range(lat):
        wide_ref[row] = grad_ref[row].astype(F32)
    for b in range(KS):

        def tile(t, totals, b=b):
            start = pl.multiple_of(t * SUB, SUB)
            grads = [wide_ref[row, pl.ds(start, SUB), :] for row in range(lat)]
            lines = [
                pad_ref[row, pl.ds(start + (SUB - RIM) + b, SUB), :] for row in range(lat + 2 * RIM)
            ]
            return tuple(
                totals[a] + functools.reduce(jnp.add, [grads[row] * lines[row + a] for row in range(lat)])
                for a in range(KS)
            )

        zero = jnp.zeros((SUB, LANES), F32)
        totals = lax.fori_loop(0, lon // SUB, tile, (zero,) * KS)
        for a in range(KS):
            out_ref[a, b : b + 1, :] = jnp.sum(totals[a], axis=0, keepdims=True) * scale


def tap_sums(before, mid, after, grad, scale):
    lat, lon, channels = mid.shape
    tokens = lat * lon
    rows = lambda n: pl.BlockSpec((n, lon, LANES), lambda i: (0, 0, i))
    return pl.pallas_call(
        functools.partial(tap_sums_body, scale),
        grid=(channels // LANES,),
        in_specs=[rows(RIM), rows(lat), rows(RIM), rows(lat)],
        out_specs=pl.BlockSpec((KS, KS, LANES), lambda i: (0, 0, i)),
        out_shape=jax.ShapeDtypeStruct((KS, KS, channels), F32),
        scratch_shapes=[
            pltpu.VMEM((lat + 2 * RIM, lon + 2 * SUB, LANES), F32),
            pltpu.VMEM((lat, lon, LANES), F32),
        ],
        compiler_params=params(20),
        cost_estimate=cost(14),
        name="tap_sums",
    )(before, mid, after, grad)


def hidden_body(n_blocks, chips_ref, n_own, n_sib, c_own, c_sib, *refs):
    shards = refs[:n_blocks]
    last_in, last_out = refs[n_blocks], refs[n_blocks + 1]
    hid_ref, grad_ref, win_ref, wout_ref, sems = refs[n_blocks + 2 :]
    size = last_in.shape[0]

    @pl.when(pl.program_id(0) == 0)
    def _():
        copies = []
        for j in range(n_blocks + 1):
            at = pl.ds(pl.multiple_of(chips_ref[j] * size, size), size)
            pair = (shards[j].at[0], shards[j].at[1]) if j < n_blocks else (last_in, last_out)
            for k, (src, dst) in enumerate(zip(pair, (win_ref, wout_ref))):
                copies.append(pltpu.make_async_copy(src, dst.at[at, :], sems.at[2 * j + k]))
        for copy in copies:
            copy.start()
        for copy in copies:
            copy.wait()

    wide = 256
    for half, (n_ref, c_ref) in enumerate(((n_own, c_own), (n_sib, c_sib))):
        for col in range(win_ref.shape[1] // wide):
            cols = slice(col * wide, (col + 1) * wide)
            pre = jnp.dot(n_ref[...], win_ref[:, cols], preferred_element_type=F32)
            back = jnp.dot(c_ref[...], wout_ref[:, cols], preferred_element_type=F32)
            area = 0.5 * (1.0 + lax.erf(pre * (1.0 / math.sqrt(2.0))))
            dens = jnp.exp(-0.5 * pre * pre) * (1.0 / math.sqrt(2.0 * math.pi))
            hid_ref[half, :, cols] = (pre * area).astype(BF16)
            grad_ref[half, :, cols] = (back * (area + pre * dens)).astype(BF16)


def hidden_step(chips, n_own, n_sib, c_own, c_sib, shards, last_in, last_out):
    tokens, channels = n_own.shape
    width = last_in.shape[1]
    high = 256
    toks = pl.BlockSpec((high, channels), lambda i, s: (i, 0))
    both = pl.BlockSpec((2, high, width), lambda i, s: (0, i, 0))
    return pl.pallas_call(
        functools.partial(hidden_body, len(shards)),
        grid_spec=pltpu.PrefetchScalarGridSpec(
            num_scalar_prefetch=1,
            grid=(tokens // high,),
            in_specs=[toks] * 4 + [pl.BlockSpec(memory_space=pl.ANY)] * (len(shards) + 2),
            out_specs=[both, both, whole((channels, width)), whole((channels, width))],
            scratch_shapes=[pltpu.SemaphoreType.DMA((2 * len(shards) + 2,))],
        ),
        out_shape=[
            jax.ShapeDtypeStruct((2, tokens, width), BF16),
            jax.ShapeDtypeStruct((2, tokens, width), BF16),
            jax.ShapeDtypeStruct((channels, width), BF16),
            jax.ShapeDtypeStruct((channels, width), BF16),
        ],
        compiler_params=params(24),
        cost_estimate=cost(11),
        name="hidden_step",
    )(chips, n_own, n_sib, c_own, c_sib, *shards, last_in, last_out)


def weight_grad_body(scale, n_own, n_sib, c_own, c_sib, hid_ref, grad_ref, out_ref):
    contract = (((0,), (0,)), ((), ()))
    for which, (own, sib, rhs) in enumerate(((n_own, n_sib, grad_ref), (c_own, c_sib, hid_ref))):
        total = lax.dot_general(own[...], rhs[0], contract, preferred_element_type=F32)
        total = total + lax.dot_general(sib[...], rhs[1], contract, preferred_element_type=F32)
        out_ref[which] = (total * scale).astype(BF16)


def weight_grads(n_own, n_sib, c_own, c_sib, hid, grad, scale):
    tokens, channels = n_own.shape
    width = hid.shape[2]
    tall = 256
    cols = pl.BlockSpec((tokens, tall), lambda i: (0, i))
    return pl.pallas_call(
        functools.partial(weight_grad_body, scale),
        grid=(channels // tall,),
        in_specs=[cols] * 4 + [whole((2, tokens, width))] * 2,
        out_specs=pl.BlockSpec((2, tall, width), lambda i: (0, i, 0)),
        out_shape=jax.ShapeDtypeStruct((2, channels, width), BF16),
        compiler_params=params(24),
        cost_estimate=cost(8),
        name="weight_grads",
    )(n_own, n_sib, c_own, c_sib, hid, grad)


def spread_first_body(lhs_ref, w_ref, out_ref):
    contract = (((1,), (1,)), ((), ()))
    for half in range(2):
        out_ref[half] = lax.dot_general(lhs_ref[half], w_ref[...], contract, preferred_element_type=F32)


def spread_last_body(lhs_ref, w_ref, prev_ref, own_ref, sib_ref):
    contract = (((1,), (1,)), ((), ()))
    own_ref[...] = prev_ref[0] + lax.dot_general(lhs_ref[0], w_ref[...], contract, preferred_element_type=F32)
    sib = prev_ref[1] + lax.dot_general(lhs_ref[1], w_ref[...], contract, preferred_element_type=F32)
    sib_ref[...] = sib.astype(BF16)


def spread(lhs, weight, prev=None):
    _, tokens, width = lhs.shape
    channels = weight.shape[0]
    high = 256
    left = pl.BlockSpec((2, high, width), lambda i: (0, i, 0))
    pair = pl.BlockSpec((2, high, channels), lambda i: (0, i, 0))
    one = pl.BlockSpec((high, channels), lambda i: (i, 0))
    common = dict(
        grid=(tokens // high,),
        compiler_params=params(24),
        cost_estimate=cost(3.5),
    )
    if prev is None:
        return pl.pallas_call(
            spread_first_body,
            in_specs=[left, whole((channels, width))],
            out_specs=pair,
            out_shape=jax.ShapeDtypeStruct((2, tokens, channels), F32),
            name="spread_first",
            **common,
        )(lhs, weight)
    return pl.pallas_call(
        spread_last_body,
        in_specs=[left, whole((channels, width)), pair],
        out_specs=[one, one],
        out_shape=[
            jax.ShapeDtypeStruct((tokens, channels), F32),
            jax.ShapeDtypeStruct((tokens, channels), BF16),
        ],
        name="spread_last",
        **common,
    )(lhs, weight, prev)


def norm_back_body(scale, own_ref, sib_ref, white_ref, inv_ref, gain_ref, out_ref, gsum_ref):
    channels = own_ref.shape[1]
    blocks = channels // LANES
    high = 16

    def tile(t, sums):
        at = pl.ds(pl.multiple_of(t * high, high), high)
        inv = inv_ref[at, :]
        terms, whites, new = [], [], []
        for j in range(blocks):
            cols = slice(j * LANES, (j + 1) * LANES)
            grad = own_ref[at, cols] + sib_ref[at, cols].astype(F32)
            white = white_ref[at, cols]
            new.append(sums[j] + jnp.sum((grad * white).reshape(high // SUB, SUB, LANES), axis=0))
            terms.append(grad * gain_ref[:, cols])
            whites.append(white)
        mean = jnp.sum(functools.reduce(jnp.add, terms), axis=-1, keepdims=True) * (1.0 / channels)
        cross = functools.reduce(jnp.add, [g * w for g, w in zip(terms, whites)])
        cross = jnp.sum(cross, axis=-1, keepdims=True) * (1.0 / channels)
        for j in range(blocks):
            cols = slice(j * LANES, (j + 1) * LANES)
            out_ref[at, cols] = (inv * (terms[j] - mean - whites[j] * cross)).astype(BF16)
        return tuple(new)

    zero = jnp.zeros((SUB, LANES), F32)
    sums = lax.fori_loop(0, own_ref.shape[0] // high, tile, (zero,) * blocks)
    for j in range(blocks):
        gsum_ref[:, j * LANES : (j + 1) * LANES] = jnp.sum(sums[j], axis=0, keepdims=True) * scale


def norm_back(own, sib, white, inv, gain, scale):
    tokens, channels = own.shape
    return pl.pallas_call(
        functools.partial(norm_back_body, scale),
        in_specs=[pl.BlockSpec(memory_space=pltpu.VMEM)] * 5,
        out_specs=[pl.BlockSpec(memory_space=pltpu.VMEM)] * 2,
        out_shape=[
            jax.ShapeDtypeStruct((tokens, channels), BF16),
            jax.ShapeDtypeStruct((1, channels), F32),
        ],
        compiler_params=params(20),
        cost_estimate=cost(3.5),
        name="norm_back",
    )(own, sib, white, inv, gain.reshape(1, channels))


def ring_order(stations):
    if stations == 8:
        return [0, 2, 4, 6, 7, 5, 3, 1]
    return list(range(stations))


def added(a, b):
    return (a.astype(F32) + b.astype(F32)).astype(BF16)


def on_device(fields, kernel, norm_gain, proj_in, proj_out, cotangent):
    lat, lon, channels = fields.shape
    row_devs = lax.axis_size("row")
    stations = row_devs // 2
    half = stations // 2
    scale = 1.0 / math.sqrt(lat * row_devs * lon)
    me = lax.axis_index("row")
    core, chip = me % 2, me // 2
    order = ring_order(stations)
    place = [order.index(i) for i in range(stations)]
    slots = [0] + [d for r in range(1, half) for d in (-r, r)] + [half]
    table = [[order[(place[p] + d) % stations] for d in slots] for p in range(stations)]
    chips = lax.dynamic_index_in_dim(jnp.array(table, jnp.int32), chip, 0, keepdims=False)
    away = lambda d: chips[slots.index(half if abs(d) == half else d)]

    def ring(step):
        return [
            (order[i] * 2 + c, order[(i + step) % stations] * 2 + c)
            for i in range(stations)
            for c in range(2)
        ]

    onward, backward = ring(1), ring(-1)
    swap = [(i, i ^ 1) for i in range(row_devs)]
    up = [(i, i + 1) for i in range(row_devs - 1)]
    down = [(i + 1, i) for i in range(row_devs - 1)]
    send = lambda value, pairs: lax.ppermute(value, "row", pairs)

    hid = proj_in.shape[1]
    mine = hid // 2
    chunks = 2
    width = mine // chunks
    size = channels // stations

    weights = jnp.stack([proj_in, proj_out.T])
    kept = lax.dynamic_slice_in_dim(weights, core * mine, mine, axis=2)
    given = lax.dynamic_slice_in_dim(weights, (1 - core) * mine, mine, axis=2)
    got = send(given, swap)
    shard = jnp.where(
        core == 0, jnp.concatenate([kept, got], axis=1), jnp.concatenate([got, kept], axis=1)
    )

    before = send(fields[lat - RIM :], up)
    after = send(fields[:RIM], down)

    def gather(part):
        on, back = part, part
        found = [part]
        for r in range(1, half):
            on, back = send(on, onward), send(back, backward)
            found += [on, back]
        last_in = send(on[0], onward)
        last_out = send(back[1], backward)
        return found, last_in, last_out

    parts = [shard[:, :, c * width : (c + 1) * width] for c in range(chunks)]
    gathered = []
    for c in range(chunks):
        part = parts[c]
        if c:
            part, _ = lax.optimization_barrier((part, gathered[-1][1]))
        gathered.append(gather(part))

    c_own = cotangent.reshape(-1, channels)
    c_sib = send(c_own, swap)
    n_own, white, inv = forward_norm(before, fields, after, kernel, norm_gain)
    n_sib = send(n_own, swap)

    def block(grads, d):
        return lax.dynamic_slice_in_dim(grads, away(d) * size, size, axis=1)

    def scatter(grads):
        on, back = None, None
        for d in range(half, 0, -1):
            ahead, behind = block(grads, d), block(grads, -d)
            if d == half:
                on, back = ahead[0], behind[1]
            elif d == half - 1:
                on = jnp.stack([added(ahead[0], on), ahead[1]])
                back = jnp.stack([behind[0], added(behind[1], back)])
            else:
                on, back = added(ahead, on), added(behind, back)
            on, back = send(on, onward), send(back, backward)
        total = block(grads, 0).astype(F32) + on.astype(F32) + back.astype(F32)
        return total.astype(BF16)

    branch = ngrad = None
    shares = []
    for c in range(chunks):
        found, last_in, last_out = gathered[c]
        hidden, pre_grad, w_in, w_out = hidden_step(
            chips, n_own, n_sib, c_own, c_sib, found, last_in, last_out
        )
        grads = weight_grads(n_own, n_sib, c_own, c_sib, hidden, pre_grad, scale)
        shares.append(scatter(grads))
        ngrad = spread(pre_grad, w_in, ngrad)
        branch = spread(hidden, w_out, branch)

    ng_sib = send(ngrad[1], swap)
    br_sib = send(branch[1], swap)
    conv_grad, gain_local = norm_back(ngrad[0], ng_sib, white, inv, norm_gain, scale)
    conv_grad = conv_grad.reshape(lat, lon, channels)
    g_before = send(conv_grad[lat - RIM :], up)
    g_after = send(conv_grad[:RIM], down)
    taps_local = tap_sums(before, fields, after, conv_grad, scale)
    result = (
        fields.astype(F32)
        + (branch[0] + br_sib.astype(F32)).reshape(fields.shape)
    ).astype(BF16)
    fields_grad = backward_conv(g_before, conv_grad, g_after, kernel, cotangent)

    small = jnp.concatenate([taps_local.reshape(KS * KS, channels), gain_local], axis=0)
    bit = 1
    while bit < row_devs:
        low = small.astype(BF16)
        other = send(low, [(i, i ^ bit) for i in range(row_devs)])
        small = low.astype(F32) + other.astype(F32)
        bit *= 2
    kernel_grad = small[: KS * KS].reshape(KS, KS, channels)
    gain_grad = small[KS * KS]

    share = jnp.concatenate(shares, axis=2)
    rows = size // 2
    keep = lax.dynamic_slice_in_dim(share, core * rows, rows, axis=1)
    give = lax.dynamic_slice_in_dim(share, (1 - core) * rows, rows, axis=1)
    got = send(give, swap)
    final = jnp.where(
        core == 0, jnp.concatenate([keep, got], axis=2), jnp.concatenate([got, keep], axis=2)
    )
    return (result, fields_grad, final[0], final[1].T, kernel_grad, gain_grad)


def solution(mesh):
    in_specs = (
        P(("grp", "row"), None, None),
        P(None, None, "grp"),
        P("grp"),
        P(("grp", "row"), None),
        P("grp", "row"),
        P(("grp", "row"), None, None),
    )
    out_specs = (
        P(("grp", "row"), None, None),
        P(("grp", "row"), None, None),
        P(("grp", "row"), None),
        P("grp", "row"),
        P(None, None, "grp"),
        P("grp"),
    )
    return jax.shard_map(
        on_device, mesh=mesh, in_specs=in_specs, out_specs=out_specs, check_vma=False
    )
```

```python
import functools
import math

import jax
import jax.numpy as jnp
from jax import lax
from jax.experimental import pallas as pl
from jax.experimental.pallas import tpu as pltpu
from jax.sharding import PartitionSpec as P

F32 = jnp.float32
BF16 = jnp.bfloat16
KS = 7
RIM = KS // 2
LANES = 128
SUB = 8
MIB = 1024 * 1024
IN_VMEM = pl.BlockSpec(memory_space=pltpu.VMEM)


def cost(micros, nbytes=0):
    return pl.CostEstimate(flops=int(micros * 1.15e9), bytes_accessed=int(nbytes), transcendentals=0)


def params(mib):
    return pltpu.CompilerParams(vmem_limit_bytes=mib * MIB)


def whole(shape):
    return pl.BlockSpec(shape, lambda *_: (0,) * len(shape))


def fill_padded(before_ref, mid_ref, after_ref, pad_ref):
    lat, lon = mid_ref.shape[0], mid_ref.shape[1]
    for row in range(lat + 2 * RIM):
        if row < RIM:
            line = before_ref[row]
        elif row < RIM + lat:
            line = mid_ref[row - RIM]
        else:
            line = after_ref[row - RIM - lat]
        line = line.astype(F32)
        pad_ref[row, pl.ds(SUB, lon), :] = line
        pad_ref[row, pl.ds(0, SUB), :] = line[lon - SUB :]
        pad_ref[row, pl.ds(SUB + lon, SUB), :] = line[:SUB]


def conv_tile(pad_ref, weight_ref, start, lat, flip):
    totals = [None] * lat
    for b in range(KS):
        lines = [
            pad_ref[row, pl.ds(start + (SUB - RIM) + b, SUB), :] for row in range(lat + 2 * RIM)
        ]
        for a in range(KS):
            index = a * KS + b
            weight = weight_ref[KS * KS - 1 - index if flip else index]
            for row in range(lat):
                term = lines[row + a] * weight
                totals[row] = term if totals[row] is None else totals[row] + term
    return totals


def spread_weights(kern_ref, weight_ref):
    taps = kern_ref[...].astype(F32)
    for a in range(KS):
        for b in range(KS):
            weight_ref[a * KS + b] = jnp.broadcast_to(taps[a, b : b + 1], (SUB, LANES))


def conv_block(before_ref, mid_ref, after_ref, kern_ref, pad_ref, weight_ref, put, flip):
    lat, lon = mid_ref.shape[0], mid_ref.shape[1]
    fill_padded(before_ref, mid_ref, after_ref, pad_ref)
    spread_weights(kern_ref, weight_ref)

    def tile(t, carry):
        start = pl.multiple_of(t * SUB, SUB)
        for row, total in enumerate(conv_tile(pad_ref, weight_ref, start, lat, flip)):
            put(row, start, total)
        return carry

    lax.fori_loop(0, lon // SUB, tile, 0, unroll=8)


def forward_first_body(before_ref, mid_ref, after_ref, kern_ref, conv_ref, pad_ref, weight_ref):
    lon = mid_ref.shape[1]

    def put(row, start, total):
        conv_ref[0, pl.ds(pl.multiple_of(row * lon + start, SUB), SUB), :] = total

    conv_block(before_ref, mid_ref, after_ref, kern_ref, pad_ref, weight_ref, put, False)


def forward_last_body(
    before_ref, mid_ref, after_ref, kern_ref, gain_ref, first_ref, normed_ref, white_ref, inv_ref, pad_ref, weight_ref, conv_ref
):
    step = pl.program_id(0)
    lon = mid_ref.shape[1]
    done, blocks = first_ref.shape[0], conv_ref.shape[0]

    def put(row, start, total):
        conv_ref[step, pl.ds(pl.multiple_of(row * lon + start, SUB), SUB), :] = total

    conv_block(before_ref, mid_ref, after_ref, kern_ref, pad_ref, weight_ref, put, False)

    @pl.when(step == blocks - 1)
    def _():
        channels = (done + blocks) * LANES
        high = 32

        def norm(t, carry):
            at = pl.ds(pl.multiple_of(t * high, high), high)
            parts = [first_ref[j, at, :] for j in range(done)]
            parts += [conv_ref[j, at, :] for j in range(blocks)]
            mean = jnp.sum(functools.reduce(jnp.add, parts), axis=-1, keepdims=True) * (1.0 / channels)
            parts = [p - mean for p in parts]
            squares = functools.reduce(jnp.add, [p * p for p in parts])
            var = jnp.sum(squares, axis=-1, keepdims=True) * (1.0 / channels)
            inv = lax.rsqrt(var + 1e-06)
            inv_ref[at, :] = jnp.broadcast_to(inv, (high, LANES))
            for j, part in enumerate(parts):
                cols = slice(j * LANES, (j + 1) * LANES)
                white = part * inv
                white_ref[at, cols] = white
                normed_ref[at, cols] = (white * gain_ref[:, cols]).astype(BF16)
            return carry

        lax.fori_loop(0, conv_ref.shape[1] // high, norm, 0)


def conv_specs(lat, lon, offset):
    rows = lambda n: pl.BlockSpec((n, lon, LANES), lambda i: (0, 0, i + offset))
    return [rows(RIM), rows(lat), rows(RIM), pl.BlockSpec((KS, KS, LANES), lambda i: (0, 0, i + offset))]


def conv_scratch(lat, lon):
    return [
        pltpu.VMEM((lat + 2 * RIM, lon + 2 * SUB, LANES), F32),
        pltpu.VMEM((KS * KS, SUB, LANES), F32),
    ]


def forward_first(before, mid, after, kernel):
    lat, lon, channels = mid.shape
    tokens, blocks = lat * lon, channels // LANES // 2
    return pl.pallas_call(
        forward_first_body,
        grid=(blocks,),
        in_specs=conv_specs(lat, lon, 0),
        out_specs=pl.BlockSpec((1, tokens, LANES), lambda i: (i, 0, 0)),
        out_shape=jax.ShapeDtypeStruct((blocks, tokens, LANES), F32),
        scratch_shapes=conv_scratch(lat, lon),
        compiler_params=params(4),
        cost_estimate=cost(5),
        name="forward_first",
    )(before, mid, after, kernel)


def forward_last(before, mid, after, kernel, gain, first):
    lat, lon, channels = mid.shape
    tokens, done = lat * lon, first.shape[0]
    blocks = channels // LANES - done
    return pl.pallas_call(
        forward_last_body,
        grid=(blocks,),
        in_specs=conv_specs(lat, lon, done) + [whole((1, channels)), IN_VMEM],
        out_specs=[IN_VMEM] * 3,
        out_shape=[
            jax.ShapeDtypeStruct((tokens, channels), BF16),
            jax.ShapeDtypeStruct((tokens, channels), F32),
            jax.ShapeDtypeStruct((tokens, LANES), F32),
        ],
        scratch_shapes=conv_scratch(lat, lon) + [pltpu.VMEM((blocks, tokens, LANES), F32)],
        compiler_params=params(5),
        cost_estimate=cost(9),
        name="forward_last",
    )(before, mid, after, kernel, gain.reshape(1, channels), first)


def backward_body(before_ref, mid_ref, after_ref, kern_ref, cot_ref, *refs):
    out_ref, pad_ref, weight_ref, sum_ref = refs[-4:]
    lat = mid_ref.shape[0]

    def put(row, start, total):
        sum_ref[row, pl.ds(start, SUB), :] = total

    conv_block(before_ref, mid_ref, after_ref, kern_ref, pad_ref, weight_ref, put, True)
    for row in range(lat):
        out_ref[row] = (cot_ref[row].astype(F32) + sum_ref[row]).astype(BF16)


def backward_conv(before, mid, after, kernel, cot, earlier=None):
    lat, lon, channels = mid.shape
    blocks = channels // LANES // 2
    offset = 0 if earlier is None else blocks
    rows = pl.BlockSpec((lat, lon, LANES), lambda i: (0, 0, i + offset))
    more = () if earlier is None else (earlier,)
    return pl.pallas_call(
        backward_body,
        grid=(blocks,),
        in_specs=conv_specs(lat, lon, offset) + [rows] + [pl.BlockSpec(memory_space=pl.ANY)] * len(more),
        out_specs=rows,
        out_shape=jax.ShapeDtypeStruct((lat, lon, channels), BF16),
        scratch_shapes=conv_scratch(lat, lon) + [pltpu.VMEM((lat, lon, LANES), F32)],
        input_output_aliases={5: 0} if more else {},
        compiler_params=params(4),
        cost_estimate=cost(6),
        name="backward_conv",
    )(before, mid, after, kernel, cot, *more)


def tap_sums_body(scale, before_ref, mid_ref, after_ref, grad_ref, out_ref, pad_ref, wide_ref):
    lat, lon = mid_ref.shape[0], mid_ref.shape[1]
    fill_padded(before_ref, mid_ref, after_ref, pad_ref)
    for row in range(lat):
        wide_ref[row] = grad_ref[row].astype(F32)
    for b in range(KS):

        def tile(t, totals, b=b):
            start = pl.multiple_of(t * SUB, SUB)
            grads = [wide_ref[row, pl.ds(start, SUB), :] for row in range(lat)]
            lines = [
                pad_ref[row, pl.ds(start + (SUB - RIM) + b, SUB), :] for row in range(lat + 2 * RIM)
            ]
            return tuple(
                totals[a] + functools.reduce(jnp.add, [grads[row] * lines[row + a] for row in range(lat)])
                for a in range(KS)
            )

        zero = jnp.zeros((SUB, LANES), F32)
        totals = lax.fori_loop(0, lon // SUB, tile, (zero,) * KS, unroll=8)
        for a in range(KS):
            out_ref[a, b : b + 1, :] = jnp.sum(totals[a], axis=0, keepdims=True) * scale


def tap_sums(before, mid, after, grad, scale):
    lat, lon, channels = mid.shape
    tokens = lat * lon
    rows = lambda n: pl.BlockSpec((n, lon, LANES), lambda i: (0, 0, i))
    return pl.pallas_call(
        functools.partial(tap_sums_body, scale),
        grid=(channels // LANES,),
        in_specs=[rows(RIM), rows(lat), rows(RIM), rows(lat)],
        out_specs=pl.BlockSpec((KS, KS, LANES), lambda i: (0, 0, i)),
        out_shape=jax.ShapeDtypeStruct((KS, KS, channels), F32),
        scratch_shapes=[
            pltpu.VMEM((lat + 2 * RIM, lon + 2 * SUB, LANES), F32),
            pltpu.VMEM((lat, lon, LANES), F32),
        ],
        compiler_params=params(4),
        cost_estimate=cost(10),
        name="tap_sums",
    )(before, mid, after, grad)


HIGH = 256


def tiles(size):
    return [slice(t, t + HIGH) for t in range(0, size, HIGH)]


def hidden_body(n_blocks, chips_ref, n_own, n_sib, c_own, c_sib, *refs):
    shards, last = refs[: n_blocks - 1], refs[n_blocks - 1 : n_blocks + 1]
    hid_ref, grad_ref, win_ref, wout_ref, sems = refs[n_blocks + 1 :]
    size = last[0].shape[0]
    copies = []
    for j in range(n_blocks):
        at = pl.ds(pl.multiple_of(chips_ref[j] * size, size), size)
        for k, target in enumerate((win_ref, wout_ref)):
            source = shards[j].at[k] if j < n_blocks - 1 else last[k]
            copies.append(pltpu.make_async_copy(source, target.at[at, :], sems.at[2 * j + k]))
    for copy in copies:
        copy.start()
    for copy in copies:
        copy.wait()
    for half, (n_ref, c_ref) in enumerate(((n_own, c_own), (n_sib, c_sib))):

        def rows(t, carry, half=half, n_ref=n_ref, c_ref=c_ref):
            at = pl.ds(pl.multiple_of(t * HIGH, HIGH), HIGH)
            for cols in tiles(win_ref.shape[1]):
                pre = jnp.dot(n_ref[at, :], win_ref[:, cols], preferred_element_type=F32)
                back = jnp.dot(c_ref[at, :], wout_ref[:, cols], preferred_element_type=F32)
                area = 0.5 * (1.0 + lax.erf(pre * (1.0 / math.sqrt(2.0))))
                dens = jnp.exp(-0.5 * pre * pre) * (1.0 / math.sqrt(2.0 * math.pi))
                hid_ref[half, at, cols] = (pre * area).astype(BF16)
                grad_ref[half, at, cols] = (back * (area + pre * dens)).astype(BF16)
            return carry

        lax.fori_loop(0, n_ref.shape[0] // HIGH, rows, 0)


def hidden_step(chips, n_own, n_sib, c_own, c_sib, shards):
    tokens, channels = n_own.shape
    width = shards[-1].shape[1]
    return pl.pallas_call(
        functools.partial(hidden_body, len(shards) - 1),
        in_specs=[pl.BlockSpec(memory_space=pltpu.SMEM)]
        + [IN_VMEM] * 4
        + [pl.BlockSpec(memory_space=pltpu.HBM)] * len(shards),
        out_specs=[IN_VMEM] * 4,
        out_shape=[
            jax.ShapeDtypeStruct((2, tokens, width), BF16),
            jax.ShapeDtypeStruct((2, tokens, width), BF16),
            jax.ShapeDtypeStruct((channels, width), BF16),
            jax.ShapeDtypeStruct((channels, width), BF16),
        ],
        scratch_shapes=[pltpu.SemaphoreType.DMA((2 * len(shards),))],
        compiler_params=params(8),
        cost_estimate=cost(17),
        name="hidden_step",
    )(chips, n_own, n_sib, c_own, c_sib, *shards)


def arrange_body(size, chips_ref, *refs):
    count = len(refs) // 2
    for source, target in zip(refs[:count], refs[count:]):
        for j in range(source.shape[1] // size):
            at = pl.ds(pl.multiple_of(chips_ref[j] * size, size), size)
            target[:, j * size : (j + 1) * size] = source[:, at]


def arrange(chips, size, values):
    if size % LANES:
        return [
            jnp.concatenate(
                [
                    lax.dynamic_slice_in_dim(v, chips[j] * size, size, axis=1)
                    for j in range(v.shape[1] // size)
                ],
                axis=1,
            )
            for v in values
        ]
    return pl.pallas_call(
        functools.partial(arrange_body, size),
        in_specs=[pl.BlockSpec(memory_space=pltpu.SMEM)] + [IN_VMEM] * len(values),
        out_specs=[IN_VMEM] * len(values),
        out_shape=[jax.ShapeDtypeStruct(v.shape, v.dtype) for v in values],
        compiler_params=params(4),
        cost_estimate=cost(2),
        name="arrange",
    )(chips, *values)


def weight_grad_body(scale, rows, n_own, n_sib, c_own, c_sib, hid_ref, grad_ref, out_ref):
    contract = (((0,), (0,)), ((), ()))
    for which, (own, sib, rhs) in enumerate(((n_own, n_sib, grad_ref), (c_own, c_sib, hid_ref))):
        for t in range(0, rows[1], LANES):
            size = min(LANES, rows[1] - t)
            at = slice(rows[0] + t, rows[0] + t + size)
            total = lax.dot_general(own[:, at], rhs[0], contract, preferred_element_type=F32)
            total = total + lax.dot_general(sib[:, at], rhs[1], contract, preferred_element_type=F32)
            out_ref[which, t : t + size, :] = (total * scale).astype(BF16)


def weight_grads(n_own, n_sib, c_own, c_sib, hid, grad, scale, rows):
    width = hid.shape[2]
    return pl.pallas_call(
        functools.partial(weight_grad_body, scale, rows),
        in_specs=[IN_VMEM] * 6,
        out_specs=IN_VMEM,
        out_shape=jax.ShapeDtypeStruct((2, rows[1], width), BF16),
        compiler_params=params(12),
        cost_estimate=cost(13 * rows[1] / n_own.shape[1]),
        name="weight_grads",
    )(n_own, n_sib, c_own, c_sib, hid, grad)


def spread_body(lhs_ref, w_ref, own_ref, sib_ref):
    contract = (((1,), (1,)), ((), ()))
    for half, out_ref in enumerate((own_ref, sib_ref)):
        for at in tiles(lhs_ref.shape[1]):
            total = lax.dot_general(lhs_ref[half, at, :], w_ref[...], contract, preferred_element_type=F32)
            out_ref[at, :] = total.astype(out_ref.dtype)


def spread(lhs, weight):
    _, tokens, width = lhs.shape
    channels = weight.shape[0]
    return pl.pallas_call(
        spread_body,
        in_specs=[IN_VMEM] * 2,
        out_specs=[IN_VMEM] * 2,
        out_shape=[
            jax.ShapeDtypeStruct((tokens, channels), F32),
            jax.ShapeDtypeStruct((tokens, channels), BF16),
        ],
        compiler_params=params(8),
        cost_estimate=cost(4.7),
        name="spread",
    )(lhs, weight)


def norm_back_body(scale, own_ref, sib_ref, white_ref, inv_ref, gain_ref, out_ref, gsum_ref):
    channels = own_ref.shape[1]
    blocks = channels // LANES
    high = 16

    def tile(t, sums):
        at = pl.ds(pl.multiple_of(t * high, high), high)
        inv = inv_ref[at, :]
        terms, whites, new = [], [], []
        for j in range(blocks):
            cols = slice(j * LANES, (j + 1) * LANES)
            grad = own_ref[at, cols] + sib_ref[at, cols].astype(F32)
            white = white_ref[at, cols]
            new.append(sums[j] + jnp.sum((grad * white).reshape(high // SUB, SUB, LANES), axis=0))
            terms.append(grad * gain_ref[:, cols])
            whites.append(white)
        mean = jnp.sum(functools.reduce(jnp.add, terms), axis=-1, keepdims=True) * (1.0 / channels)
        cross = functools.reduce(jnp.add, [g * w for g, w in zip(terms, whites)])
        cross = jnp.sum(cross, axis=-1, keepdims=True) * (1.0 / channels)
        for j in range(blocks):
            cols = slice(j * LANES, (j + 1) * LANES)
            out_ref[at, cols] = (inv * (terms[j] - mean - whites[j] * cross)).astype(BF16)
        return tuple(new)

    zero = jnp.zeros((SUB, LANES), F32)
    sums = lax.fori_loop(0, own_ref.shape[0] // high, tile, (zero,) * blocks)
    for j in range(blocks):
        gsum_ref[:, j * LANES : (j + 1) * LANES] = jnp.sum(sums[j], axis=0, keepdims=True) * scale


def norm_back(own, sib, white, inv, gain, scale):
    tokens, channels = own.shape
    return pl.pallas_call(
        functools.partial(norm_back_body, scale),
        in_specs=[pl.BlockSpec(memory_space=pltpu.VMEM)] * 5,
        out_specs=[pl.BlockSpec(memory_space=pltpu.VMEM)] * 2,
        out_shape=[
            jax.ShapeDtypeStruct((tokens, channels), BF16),
            jax.ShapeDtypeStruct((1, channels), F32),
        ],
        compiler_params=params(4),
        cost_estimate=cost(3.5),
        name="norm_back",
    )(own, sib, white, inv, gain.reshape(1, channels))


def ring_order(stations):
    if stations == 8:
        return [0, 2, 4, 6, 7, 5, 3, 1]
    return list(range(stations))


def added(a, b):
    return (a.astype(F32) + b.astype(F32)).astype(BF16)


def on_device(fields, kernel, norm_gain, proj_in, proj_out, cotangent):
    lat, lon, channels = fields.shape
    row_devs = lax.axis_size("row")
    stations = row_devs // 2
    half = stations // 2
    scale = 1.0 / math.sqrt(lat * row_devs * lon)
    me = lax.axis_index("row")
    core, chip = me % 2, me // 2
    order = ring_order(stations)
    place = [order.index(i) for i in range(stations)]
    slots = [0] + [d for r in range(1, half) for d in (-r, r)] + [half]
    table = [[order[(place[p] + d) % stations] for d in slots] for p in range(stations)]
    chips = lax.dynamic_index_in_dim(jnp.array(table, jnp.int32), chip, 0, keepdims=False)
    leaving = [half] + [d for r in range(half - 1, 0, -1) for d in (r, -r)] + [0]
    table = [[order[(place[p] + d) % stations] for d in leaving] for p in range(stations)]
    leave = lax.dynamic_index_in_dim(jnp.array(table, jnp.int32), chip, 0, keepdims=False)

    swap = [(i, i ^ 1) for i in range(row_devs)]
    up = [(i, i + 1) for i in range(row_devs - 1)]
    down = [(i + 1, i) for i in range(row_devs - 1)]
    send = lambda value, pairs: lax.ppermute(value, "row", pairs)

    def rims_sent(value):
        last, first = value[lat - RIM :], value[:RIM]
        if stations != 8:
            return send(last, up), send(first, down)
        above = send(last, [p for p in up if p != (11, 12)])
        below = send(first, [p for p in down if p != (4, 3)])
        return above, below, send(jnp.where(core == 0, first, last), [(11, 9), (4, 6)])

    def rims_passed(rims):
        return (*rims[:2], *(send(r, [(9, 12), (6, 3)]) for r in rims[2:]))

    def rims_got(rims):
        if stations != 8:
            return rims
        above, below, far = rims
        return jnp.where(me == 12, far, above), jnp.where(me == 3, far, below)

    def ring(step):
        return [
            (order[i] * 2 + c, order[(i + step) % stations] * 2 + c)
            for i in range(stations)
            for c in range(2)
        ]

    onward, backward = ring(1), ring(-1)

    hid = proj_in.shape[1]
    mine = hid // 2
    size = channels // stations

    weights = jnp.stack([proj_in, proj_out.T])
    kept = lax.dynamic_slice_in_dim(weights, core * mine, mine, axis=2)
    given = lax.dynamic_slice_in_dim(weights, (1 - core) * mine, mine, axis=2)
    got = send(given, swap)
    shard = jnp.where(
        core == 0, jnp.concatenate([kept, got], axis=1), jnp.concatenate([got, kept], axis=1)
    )

    fence = lax.optimization_barrier

    class Gather:
        def __init__(self, part):
            self.found, self.left = [part], half
            self.pair = part, part

        def step(self):
            self.left -= 1
            on, back = self.pair
            if not self.left:
                on, back = on[0], back[1]
            self.pair = send(on, onward), send(back, backward)
            return self.pair

        def arrived(self, pair):
            self.pair = pair
            self.found += pair

    class Scatter:
        def __init__(self):
            self.d = half
            self.blocks = {}
            self.pair = None

        def step(self):
            d = self.d
            self.d = d - 1
            if d == half:
                on, back = self.blocks[d][0], self.blocks[d][1]
            else:
                on, back = self.blocks[d], self.blocks[-d]
                if d == half - 1:
                    on = jnp.stack([added(on[0], self.pair[0]), on[1]])
                    back, come, on = fence((back, self.pair[1], on))
                    back = jnp.stack([back[0], added(back[1], come)])
                else:
                    on = added(on, self.pair[0])
                    back, come, on = fence((back, self.pair[1], on))
                    back = added(back, come)
            self.pair = send(on, onward), send(back, backward)
            return self.pair

        def arrived(self, pair):
            self.pair = pair

        def total(self):
            total = self.blocks[0].astype(F32) + self.pair[0].astype(F32) + self.pair[1].astype(F32)
            return total.astype(BF16)

    def joined(value, bit):
        low = value.astype(BF16)
        return low, send(low, [(i, i ^ bit) for i in range(row_devs)])

    def summed(pair):
        return pair[0].astype(F32) + pair[1].astype(F32)

    c_own = cotangent.reshape(-1, channels)
    load, sums = Gather(shard), Scatter()
    pairs = load.step()
    rims = rims_sent(fields)
    c_sib = send(c_own, swap)
    pairs = fence(pairs)
    load.arrived(pairs)
    pairs = load.step()
    pairs, rims, c_sib = fence((pairs, rims_passed(rims), c_sib))
    load.arrived(pairs)
    for _ in range(half - 4):
        load.arrived(fence(load.step()))
    pairs = load.step()
    before, after = rims_got(rims)
    conv = forward_first(before, fields, after, kernel)
    n_own, white, inv = forward_last(before, fields, after, kernel, norm_gain, conv)
    pairs, n_own = fence((pairs, n_own))
    load.arrived(pairs)
    pairs = load.step()
    n_sib = send(n_own, swap)
    order_in = arrange(leave, size, (n_own, n_sib, c_own, c_sib))
    pairs, order_in, n_sib = fence((pairs, order_in, n_sib))
    load.arrived(pairs)
    hidden, pre_grad, w_in, w_out = hidden_step(
        chips, n_own, n_sib, c_own, c_sib, load.found
    )
    early = 3 * size

    def keep(part, names):
        for k, d in enumerate(names):
            sums.blocks[d] = part[:, k * size : (k + 1) * size]

    parts = weight_grads(*order_in, hidden, pre_grad, scale, (0, early))
    parts, hidden, pre_grad, order_in = fence((parts, hidden, pre_grad, order_in))
    keep(parts, leaving[:3])
    pairs = sums.step()
    parts = weight_grads(*order_in, hidden, pre_grad, scale, (early, channels - early))
    pre_grad, parts = fence((pre_grad, parts))
    ngrad = spread(pre_grad, w_in)
    pairs, parts, hidden, ngrad = fence((pairs, parts, hidden, ngrad))
    keep(parts, leaving[3:])
    sums.arrived(pairs)
    pairs = sums.step()
    ng_sib = send(ngrad[1], swap)
    branch = spread(hidden, w_out)
    ng_sib, branch = fence((ng_sib, branch))
    conv_grad, gain_local = norm_back(ngrad[0], ng_sib, white, inv, norm_gain, scale)
    conv_grad = fence(conv_grad).reshape(lat, lon, channels)
    rims = send(conv_grad[lat - RIM :], up), send(conv_grad[:RIM], down)
    taps_local = tap_sums(before, fields, after, conv_grad, scale)
    pairs, rims, taps_local, branch = fence((pairs, rims, taps_local, branch))
    sums.arrived(pairs)
    for _ in range(half - 4):
        sums.arrived(fence(sums.step()))
    pairs = sums.step()
    small = joined(jnp.concatenate([taps_local.reshape(KS * KS, channels), gain_local], axis=0), 4)
    rims, small = fence((rims, small))
    g_before, g_after = rims
    small = joined(summed(small), 8)
    fields_grad = backward_conv(g_before, conv_grad, g_after, kernel, cotangent)
    fields_grad = backward_conv(g_before, conv_grad, g_after, kernel, cotangent, fields_grad)
    br_sib = send(branch[1], swap)
    pairs, fields_grad, br_sib, small = fence((pairs, fields_grad, br_sib, small))
    sums.arrived(pairs)
    pairs = sums.step()
    small = joined(summed(small), 2)
    result = (
        fields.astype(F32) + (branch[0] + br_sib.astype(F32)).reshape(fields.shape)
    ).astype(BF16)
    small, pairs, result = fence((small, pairs, result))
    sums.arrived(pairs)
    for bit in [1 << k for k in range(4, row_devs.bit_length() - 1)] + [1]:
        small = joined(summed(small), bit)
    small = summed(small)
    kernel_grad = small[: KS * KS].reshape(KS, KS, channels)
    gain_grad = small[KS * KS]

    share = sums.total()
    rows = size // 2
    stay = lax.dynamic_slice_in_dim(share, core * rows, rows, axis=1)
    give = lax.dynamic_slice_in_dim(share, (1 - core) * rows, rows, axis=1)
    got = send(give, swap)
    final = jnp.where(
        core == 0, jnp.concatenate([stay, got], axis=2), jnp.concatenate([got, stay], axis=2)
    )
    return (result, fields_grad, final[0], final[1].T, kernel_grad, gain_grad)


def solution(mesh):
    in_specs = (
        P(("grp", "row"), None, None),
        P(None, None, "grp"),
        P("grp"),
        P(("grp", "row"), None),
        P("grp", "row"),
        P(("grp", "row"), None, None),
    )
    out_specs = (
        P(("grp", "row"), None, None),
        P(("grp", "row"), None, None),
        P(("grp", "row"), None),
        P("grp", "row"),
        P(None, None, "grp"),
        P("grp"),
    )
    return jax.shard_map(
        on_device, mesh=mesh, in_specs=in_specs, out_specs=out_specs, check_vma=False
    )
```

```python
import functools
import math

import jax
import jax.numpy as jnp
from jax import lax
from jax.experimental import pallas as pl
from jax.experimental.pallas import tpu as pltpu
from jax.sharding import PartitionSpec as P

F32 = jnp.float32
BF16 = jnp.bfloat16
KS = 7
RIM = KS // 2
LANES = 128
SUB = 8
MIB = 1024 * 1024
IN_VMEM = pl.BlockSpec(memory_space=pltpu.VMEM)


def cost(micros, nbytes=0):
    return pl.CostEstimate(flops=int(micros * 1.15e9), bytes_accessed=int(nbytes), transcendentals=0)


def params(mib):
    return pltpu.CompilerParams(vmem_limit_bytes=mib * MIB)


def whole(shape):
    return pl.BlockSpec(shape, lambda *_: (0,) * len(shape))


def fill_padded(before_ref, mid_ref, after_ref, pad_ref):
    lat, lon = mid_ref.shape[0], mid_ref.shape[1]
    for row in range(lat + 2 * RIM):
        if row < RIM:
            line = before_ref[row]
        elif row < RIM + lat:
            line = mid_ref[row - RIM]
        else:
            line = after_ref[row - RIM - lat]
        line = line.astype(F32)
        pad_ref[row, pl.ds(SUB, lon), :] = line
        pad_ref[row, pl.ds(0, SUB), :] = line[lon - SUB :]
        pad_ref[row, pl.ds(SUB + lon, SUB), :] = line[:SUB]


def conv_tile(pad_ref, weight_ref, start, lat, flip):
    totals = [None] * lat
    for b in range(KS):
        lines = [
            pad_ref[row, pl.ds(start + (SUB - RIM) + b, SUB), :] for row in range(lat + 2 * RIM)
        ]
        for a in range(KS):
            index = a * KS + b
            weight = weight_ref[KS * KS - 1 - index if flip else index]
            for row in range(lat):
                term = lines[row + a] * weight
                totals[row] = term if totals[row] is None else totals[row] + term
    return totals


def spread_weights(kern_ref, weight_ref):
    taps = kern_ref[...].astype(F32)
    for a in range(KS):
        for b in range(KS):
            weight_ref[a * KS + b] = jnp.broadcast_to(taps[a, b : b + 1], (SUB, LANES))


def conv_block(before_ref, mid_ref, after_ref, kern_ref, pad_ref, weight_ref, put, flip):
    lat, lon = mid_ref.shape[0], mid_ref.shape[1]
    fill_padded(before_ref, mid_ref, after_ref, pad_ref)
    spread_weights(kern_ref, weight_ref)

    def tile(t, carry):
        start = pl.multiple_of(t * SUB, SUB)
        for row, total in enumerate(conv_tile(pad_ref, weight_ref, start, lat, flip)):
            put(row, start, total)
        return carry

    lax.fori_loop(0, lon // SUB, tile, 0, unroll=8)


def forward_first_body(before_ref, mid_ref, after_ref, kern_ref, conv_ref, pad_ref, weight_ref):
    lon = mid_ref.shape[1]

    def put(row, start, total):
        conv_ref[0, pl.ds(pl.multiple_of(row * lon + start, SUB), SUB), :] = total

    conv_block(before_ref, mid_ref, after_ref, kern_ref, pad_ref, weight_ref, put, False)


def forward_last_body(
    before_ref, mid_ref, after_ref, kern_ref, gain_ref, first_ref, normed_ref, white_ref, inv_ref, pad_ref, weight_ref, conv_ref
):
    step = pl.program_id(0)
    lon = mid_ref.shape[1]
    done, blocks = first_ref.shape[0], conv_ref.shape[0]

    def put(row, start, total):
        conv_ref[step, pl.ds(pl.multiple_of(row * lon + start, SUB), SUB), :] = total

    conv_block(before_ref, mid_ref, after_ref, kern_ref, pad_ref, weight_ref, put, False)

    @pl.when(step == blocks - 1)
    def _():
        channels = (done + blocks) * LANES
        high = 32

        def norm(t, carry):
            at = pl.ds(pl.multiple_of(t * high, high), high)
            parts = [first_ref[j, at, :] for j in range(done)]
            parts += [conv_ref[j, at, :] for j in range(blocks)]
            mean = jnp.sum(functools.reduce(jnp.add, parts), axis=-1, keepdims=True) * (1.0 / channels)
            parts = [p - mean for p in parts]
            squares = functools.reduce(jnp.add, [p * p for p in parts])
            var = jnp.sum(squares, axis=-1, keepdims=True) * (1.0 / channels)
            inv = lax.rsqrt(var + 1e-06)
            inv_ref[at, :] = jnp.broadcast_to(inv, (high, LANES))
            for j, part in enumerate(parts):
                cols = slice(j * LANES, (j + 1) * LANES)
                white = part * inv
                white_ref[at, cols] = white
                normed_ref[at, cols] = (white * gain_ref[:, cols]).astype(BF16)
            return carry

        lax.fori_loop(0, conv_ref.shape[1] // high, norm, 0)


def conv_specs(lat, lon, offset):
    rows = lambda n: pl.BlockSpec((n, lon, LANES), lambda i: (0, 0, i + offset))
    return [rows(RIM), rows(lat), rows(RIM), pl.BlockSpec((KS, KS, LANES), lambda i: (0, 0, i + offset))]


def conv_scratch(lat, lon):
    return [
        pltpu.VMEM((lat + 2 * RIM, lon + 2 * SUB, LANES), F32),
        pltpu.VMEM((KS * KS, SUB, LANES), F32),
    ]


def forward_first(before, mid, after, kernel):
    lat, lon, channels = mid.shape
    tokens, blocks = lat * lon, channels // LANES // 2
    return pl.pallas_call(
        forward_first_body,
        grid=(blocks,),
        in_specs=conv_specs(lat, lon, 0),
        out_specs=pl.BlockSpec((1, tokens, LANES), lambda i: (i, 0, 0)),
        out_shape=jax.ShapeDtypeStruct((blocks, tokens, LANES), F32),
        scratch_shapes=conv_scratch(lat, lon),
        compiler_params=params(4),
        cost_estimate=cost(5),
        name="forward_first",
    )(before, mid, after, kernel)


def forward_last(before, mid, after, kernel, gain, first):
    lat, lon, channels = mid.shape
    tokens, done = lat * lon, first.shape[0]
    blocks = channels // LANES - done
    return pl.pallas_call(
        forward_last_body,
        grid=(blocks,),
        in_specs=conv_specs(lat, lon, done) + [whole((1, channels)), IN_VMEM],
        out_specs=[IN_VMEM] * 3,
        out_shape=[
            jax.ShapeDtypeStruct((tokens, channels), BF16),
            jax.ShapeDtypeStruct((tokens, channels), F32),
            jax.ShapeDtypeStruct((tokens, LANES), F32),
        ],
        scratch_shapes=conv_scratch(lat, lon) + [pltpu.VMEM((blocks, tokens, LANES), F32)],
        compiler_params=params(5),
        cost_estimate=cost(9),
        name="forward_last",
    )(before, mid, after, kernel, gain.reshape(1, channels), first)


def backward_body(before_ref, mid_ref, after_ref, kern_ref, cot_ref, *refs):
    out_ref, pad_ref, weight_ref, sum_ref = refs[-4:]
    lat = mid_ref.shape[0]

    def put(row, start, total):
        sum_ref[row, pl.ds(start, SUB), :] = total

    conv_block(before_ref, mid_ref, after_ref, kern_ref, pad_ref, weight_ref, put, True)
    for row in range(lat):
        out_ref[row] = (cot_ref[row].astype(F32) + sum_ref[row]).astype(BF16)


def backward_conv(before, mid, after, kernel, cot, earlier=None):
    lat, lon, channels = mid.shape
    blocks = channels // LANES // 2
    offset = 0 if earlier is None else blocks
    rows = pl.BlockSpec((lat, lon, LANES), lambda i: (0, 0, i + offset))
    more = () if earlier is None else (earlier,)
    return pl.pallas_call(
        backward_body,
        grid=(blocks,),
        in_specs=conv_specs(lat, lon, offset) + [rows] + [pl.BlockSpec(memory_space=pl.ANY)] * len(more),
        out_specs=rows,
        out_shape=jax.ShapeDtypeStruct((lat, lon, channels), BF16),
        scratch_shapes=conv_scratch(lat, lon) + [pltpu.VMEM((lat, lon, LANES), F32)],
        input_output_aliases={5: 0} if more else {},
        compiler_params=params(4),
        cost_estimate=cost(6),
        name="backward_conv",
    )(before, mid, after, kernel, cot, *more)


def tap_sums_body(scale, before_ref, mid_ref, after_ref, grad_ref, out_ref, pad_ref, wide_ref):
    lat, lon = mid_ref.shape[0], mid_ref.shape[1]
    fill_padded(before_ref, mid_ref, after_ref, pad_ref)
    for row in range(lat):
        wide_ref[row] = grad_ref[row].astype(F32)
    for b in range(KS):

        def tile(t, totals, b=b):
            start = pl.multiple_of(t * SUB, SUB)
            grads = [wide_ref[row, pl.ds(start, SUB), :] for row in range(lat)]
            lines = [
                pad_ref[row, pl.ds(start + (SUB - RIM) + b, SUB), :] for row in range(lat + 2 * RIM)
            ]
            return tuple(
                totals[a] + functools.reduce(jnp.add, [grads[row] * lines[row + a] for row in range(lat)])
                for a in range(KS)
            )

        zero = jnp.zeros((SUB, LANES), F32)
        totals = lax.fori_loop(0, lon // SUB, tile, (zero,) * KS, unroll=8)
        for a in range(KS):
            out_ref[a, b : b + 1, :] = jnp.sum(totals[a], axis=0, keepdims=True) * scale


def tap_sums(before, mid, after, grad, scale):
    lat, lon, channels = mid.shape
    tokens = lat * lon
    rows = lambda n: pl.BlockSpec((n, lon, LANES), lambda i: (0, 0, i))
    return pl.pallas_call(
        functools.partial(tap_sums_body, scale),
        grid=(channels // LANES,),
        in_specs=[rows(RIM), rows(lat), rows(RIM), rows(lat)],
        out_specs=pl.BlockSpec((KS, KS, LANES), lambda i: (0, 0, i)),
        out_shape=jax.ShapeDtypeStruct((KS, KS, channels), F32),
        scratch_shapes=[
            pltpu.VMEM((lat + 2 * RIM, lon + 2 * SUB, LANES), F32),
            pltpu.VMEM((lat, lon, LANES), F32),
        ],
        compiler_params=params(4),
        cost_estimate=cost(10),
        name="tap_sums",
    )(before, mid, after, grad)


HIGH = 256


def tiles(size):
    return [slice(t, t + HIGH) for t in range(0, size, HIGH)]


def hidden_body(n_blocks, chips_ref, n_own, n_sib, c_own, c_sib, *refs):
    shards, last = refs[: n_blocks - 1], refs[n_blocks - 1 : n_blocks + 1]
    hid_ref, grad_ref, win_ref, wout_ref, sems = refs[n_blocks + 1 :]
    size = last[0].shape[0]
    copies = []
    for j in range(n_blocks):
        at = pl.ds(pl.multiple_of(chips_ref[j] * size, size), size)
        for k, target in enumerate((win_ref, wout_ref)):
            source = shards[j].at[k] if j < n_blocks - 1 else last[k]
            copies.append(pltpu.make_async_copy(source, target.at[at, :], sems.at[2 * j + k]))
    for copy in copies:
        copy.start()
    for copy in copies:
        copy.wait()
    for half, (n_ref, c_ref) in enumerate(((n_own, c_own), (n_sib, c_sib))):

        def rows(t, carry, half=half, n_ref=n_ref, c_ref=c_ref):
            at = pl.ds(pl.multiple_of(t * HIGH, HIGH), HIGH)
            for cols in tiles(win_ref.shape[1]):
                pre = jnp.dot(n_ref[at, :], win_ref[:, cols], preferred_element_type=F32)
                back = jnp.dot(c_ref[at, :], wout_ref[:, cols], preferred_element_type=F32)
                area = 0.5 * (1.0 + lax.erf(pre * (1.0 / math.sqrt(2.0))))
                dens = jnp.exp(-0.5 * pre * pre) * (1.0 / math.sqrt(2.0 * math.pi))
                hid_ref[half, at, cols] = (pre * area).astype(BF16)
                grad_ref[half, at, cols] = (back * (area + pre * dens)).astype(BF16)
            return carry

        lax.fori_loop(0, n_ref.shape[0] // HIGH, rows, 0)


def hidden_step(chips, n_own, n_sib, c_own, c_sib, shards):
    tokens, channels = n_own.shape
    width = shards[-1].shape[1]
    return pl.pallas_call(
        functools.partial(hidden_body, len(shards) - 1),
        in_specs=[pl.BlockSpec(memory_space=pltpu.SMEM)]
        + [IN_VMEM] * 4
        + [pl.BlockSpec(memory_space=pltpu.HBM)] * len(shards),
        out_specs=[IN_VMEM] * 4,
        out_shape=[
            jax.ShapeDtypeStruct((2, tokens, width), BF16),
            jax.ShapeDtypeStruct((2, tokens, width), BF16),
            jax.ShapeDtypeStruct((channels, width), BF16),
            jax.ShapeDtypeStruct((channels, width), BF16),
        ],
        scratch_shapes=[pltpu.SemaphoreType.DMA((2 * len(shards),))],
        compiler_params=params(8),
        cost_estimate=cost(17),
        name="hidden_step",
    )(chips, n_own, n_sib, c_own, c_sib, *shards)


def arrange_body(size, chips_ref, *refs):
    count = len(refs) // 2
    for source, target in zip(refs[:count], refs[count:]):
        for j in range(source.shape[1] // size):
            at = pl.ds(pl.multiple_of(chips_ref[j] * size, size), size)
            target[:, j * size : (j + 1) * size] = source[:, at]


def arrange(chips, size, values):
    if size % LANES:
        return [
            jnp.concatenate(
                [
                    lax.dynamic_slice_in_dim(v, chips[j] * size, size, axis=1)
                    for j in range(v.shape[1] // size)
                ],
                axis=1,
            )
            for v in values
        ]
    return pl.pallas_call(
        functools.partial(arrange_body, size),
        in_specs=[pl.BlockSpec(memory_space=pltpu.SMEM)] + [IN_VMEM] * len(values),
        out_specs=[IN_VMEM] * len(values),
        out_shape=[jax.ShapeDtypeStruct(v.shape, v.dtype) for v in values],
        compiler_params=params(4),
        cost_estimate=cost(2),
        name="arrange",
    )(chips, *values)


def weight_grad_body(scale, size, first, n_own, n_sib, c_own, c_sib, hid_ref, grad_ref, *outs):
    contract = (((0,), (0,)), ((), ()))
    for k, out_ref in enumerate(outs):
        at = slice((first + k) * size, (first + k + 1) * size)
        for which, (own, sib, rhs) in enumerate(((n_own, n_sib, grad_ref), (c_own, c_sib, hid_ref))):
            total = lax.dot_general(own[:, at], rhs[0], contract, preferred_element_type=F32)
            total = total + lax.dot_general(sib[:, at], rhs[1], contract, preferred_element_type=F32)
            out_ref[which] = (total * scale).astype(BF16)


def weight_grads(n_own, n_sib, c_own, c_sib, hid, grad, scale, size, first, count):
    width = hid.shape[2]
    shape = jax.ShapeDtypeStruct((2, size, width), BF16)
    return pl.pallas_call(
        functools.partial(weight_grad_body, scale, size, first),
        in_specs=[IN_VMEM] * 6,
        out_specs=[IN_VMEM] * count,
        out_shape=[shape] * count,
        compiler_params=params(12),
        cost_estimate=cost(9 * size * count / n_own.shape[1]),
        name="weight_grads",
    )(n_own, n_sib, c_own, c_sib, hid, grad)


def spread_body(lhs_ref, w_ref, own_ref, sib_ref):
    contract = (((1,), (1,)), ((), ()))
    for half, out_ref in enumerate((own_ref, sib_ref)):
        for at in tiles(lhs_ref.shape[1]):
            total = lax.dot_general(lhs_ref[half, at, :], w_ref[...], contract, preferred_element_type=F32)
            out_ref[at, :] = total.astype(out_ref.dtype)


def spread(lhs, weight):
    _, tokens, width = lhs.shape
    channels = weight.shape[0]
    return pl.pallas_call(
        spread_body,
        in_specs=[IN_VMEM] * 2,
        out_specs=[IN_VMEM] * 2,
        out_shape=[
            jax.ShapeDtypeStruct((tokens, channels), F32),
            jax.ShapeDtypeStruct((tokens, channels), BF16),
        ],
        compiler_params=params(8),
        cost_estimate=cost(4.7),
        name="spread",
    )(lhs, weight)


def norm_back_body(scale, own_ref, sib_ref, white_ref, inv_ref, gain_ref, out_ref, gsum_ref):
    channels = own_ref.shape[1]
    blocks = channels // LANES
    high = 16

    def tile(t, sums):
        at = pl.ds(pl.multiple_of(t * high, high), high)
        inv = inv_ref[at, :]
        terms, whites, new = [], [], []
        for j in range(blocks):
            cols = slice(j * LANES, (j + 1) * LANES)
            grad = own_ref[at, cols] + sib_ref[at, cols].astype(F32)
            white = white_ref[at, cols]
            new.append(sums[j] + jnp.sum((grad * white).reshape(high // SUB, SUB, LANES), axis=0))
            terms.append(grad * gain_ref[:, cols])
            whites.append(white)
        mean = jnp.sum(functools.reduce(jnp.add, terms), axis=-1, keepdims=True) * (1.0 / channels)
        cross = functools.reduce(jnp.add, [g * w for g, w in zip(terms, whites)])
        cross = jnp.sum(cross, axis=-1, keepdims=True) * (1.0 / channels)
        for j in range(blocks):
            cols = slice(j * LANES, (j + 1) * LANES)
            out_ref[at, cols] = (inv * (terms[j] - mean - whites[j] * cross)).astype(BF16)
        return tuple(new)

    zero = jnp.zeros((SUB, LANES), F32)
    sums = lax.fori_loop(0, own_ref.shape[0] // high, tile, (zero,) * blocks)
    for j in range(blocks):
        gsum_ref[:, j * LANES : (j + 1) * LANES] = jnp.sum(sums[j], axis=0, keepdims=True) * scale


def norm_back(own, sib, white, inv, gain, scale):
    tokens, channels = own.shape
    return pl.pallas_call(
        functools.partial(norm_back_body, scale),
        in_specs=[pl.BlockSpec(memory_space=pltpu.VMEM)] * 5,
        out_specs=[pl.BlockSpec(memory_space=pltpu.VMEM)] * 2,
        out_shape=[
            jax.ShapeDtypeStruct((tokens, channels), BF16),
            jax.ShapeDtypeStruct((1, channels), F32),
        ],
        compiler_params=params(4),
        cost_estimate=cost(3.5),
        name="norm_back",
    )(own, sib, white, inv, gain.reshape(1, channels))


def ring_order(stations):
    if stations == 8:
        return [0, 2, 4, 6, 7, 5, 3, 1]
    return list(range(stations))


def added(a, b):
    return (a.astype(F32) + b.astype(F32)).astype(BF16)


def on_device(fields, kernel, norm_gain, proj_in, proj_out, cotangent):
    lat, lon, channels = fields.shape
    row_devs = lax.axis_size("row")
    stations = row_devs // 2
    half = stations // 2
    scale = 1.0 / math.sqrt(lat * row_devs * lon)
    me = lax.axis_index("row")
    core, chip = me % 2, me // 2
    order = ring_order(stations)
    place = [order.index(i) for i in range(stations)]
    slots = [0] + [d for r in range(1, half) for d in (-r, r)] + [half]
    table = [[order[(place[p] + d) % stations] for d in slots] for p in range(stations)]
    chips = lax.dynamic_index_in_dim(jnp.array(table, jnp.int32), chip, 0, keepdims=False)
    leaving = [half] + [d for r in range(half - 1, 0, -1) for d in (r, -r)] + [0]
    table = [[order[(place[p] + d) % stations] for d in leaving] for p in range(stations)]
    leave = lax.dynamic_index_in_dim(jnp.array(table, jnp.int32), chip, 0, keepdims=False)

    swap = [(i, i ^ 1) for i in range(row_devs)]
    up = [(i, i + 1) for i in range(row_devs - 1)]
    down = [(i + 1, i) for i in range(row_devs - 1)]
    send = lambda value, pairs: lax.ppermute(value, "row", pairs)

    def rims_sent(value):
        last, first = value[lat - RIM :], value[:RIM]
        if stations != 8:
            return send(last, up), send(first, down)
        above = send(last, [p for p in up if p != (11, 12)])
        below = send(first, [p for p in down if p != (4, 3)])
        return above, below, send(jnp.where(core == 0, first, last), [(11, 9), (4, 6)])

    def rims_passed(rims):
        return (*rims[:2], *(send(r, [(9, 12), (6, 3)]) for r in rims[2:]))

    def rims_got(rims):
        if stations != 8:
            return rims
        above, below, far = rims
        return jnp.where(me == 12, far, above), jnp.where(me == 3, far, below)

    def ring(step):
        return [
            (order[i] * 2 + c, order[(i + step) % stations] * 2 + c)
            for i in range(stations)
            for c in range(2)
        ]

    onward, backward = ring(1), ring(-1)

    hid = proj_in.shape[1]
    mine = hid // 2
    size = channels // stations

    weights = jnp.stack([proj_in, proj_out.T])
    kept = lax.dynamic_slice_in_dim(weights, core * mine, mine, axis=2)
    given = lax.dynamic_slice_in_dim(weights, (1 - core) * mine, mine, axis=2)
    got = send(given, swap)
    shard = jnp.where(
        core == 0, jnp.concatenate([kept, got], axis=1), jnp.concatenate([got, kept], axis=1)
    )

    fence = lax.optimization_barrier

    class Gather:
        def __init__(self, part):
            self.found, self.left = [part], half
            self.pair = part, part

        def step(self):
            self.left -= 1
            on, back = self.pair
            if not self.left:
                on, back = on[0], back[1]
            self.pair = send(on, onward), send(back, backward)
            return self.pair

        def arrived(self, pair):
            self.pair = pair
            self.found += pair

    class Scatter:
        def __init__(self):
            self.d = half
            self.blocks = {}
            self.pair = None

        def step(self):
            d = self.d
            self.d = d - 1
            if d == half:
                on, back = self.blocks[d][0], self.blocks[d][1]
            else:
                on, back = self.blocks[d], self.blocks[-d]
                if d == half - 1:
                    on = jnp.stack([added(on[0], self.pair[0]), on[1]])
                    back, come, on = fence((back, self.pair[1], on))
                    back = jnp.stack([back[0], added(back[1], come)])
                else:
                    on = added(on, self.pair[0])
                    back, come, on = fence((back, self.pair[1], on))
                    back = added(back, come)
            self.pair = send(on, onward), send(back, backward)
            return self.pair

        def arrived(self, pair):
            self.pair = pair

        def total(self):
            total = self.blocks[0].astype(F32) + self.pair[0].astype(F32) + self.pair[1].astype(F32)
            return total.astype(BF16)

    def joined(value, bit):
        low = value.astype(BF16)
        return low, send(low, [(i, i ^ bit) for i in range(row_devs)])

    def summed(pair):
        return pair[0].astype(F32) + pair[1].astype(F32)

    c_own = cotangent.reshape(-1, channels)
    load, sums = Gather(shard), Scatter()
    pairs = load.step()
    rims = rims_sent(fields)
    c_sib = send(c_own, swap)
    pairs = fence(pairs)
    load.arrived(pairs)
    pairs = load.step()
    pairs, rims, c_sib = fence((pairs, rims_passed(rims), c_sib))
    load.arrived(pairs)
    for _ in range(half - 4):
        load.arrived(fence(load.step()))
    pairs = load.step()
    before, after = rims_got(rims)
    conv = forward_first(before, fields, after, kernel)
    n_own, white, inv = forward_last(before, fields, after, kernel, norm_gain, conv)
    pairs, n_own = fence((pairs, n_own))
    load.arrived(pairs)
    pairs = load.step()
    n_sib = send(n_own, swap)
    order_in = arrange(leave, size, (n_own, n_sib, c_own, c_sib))
    pairs, order_in, n_sib = fence((pairs, order_in, n_sib))
    load.arrived(pairs)
    hidden, pre_grad, w_in, w_out = hidden_step(
        chips, n_own, n_sib, c_own, c_sib, load.found
    )
    early = 3

    def keep(blocks, names):
        sums.blocks.update(zip(names, blocks))

    blocks = weight_grads(*order_in, hidden, pre_grad, scale, size, 0, early)
    blocks, hidden, pre_grad, order_in = fence((blocks, hidden, pre_grad, order_in))
    keep(blocks, leaving[:early])
    pairs = sums.step()
    blocks = weight_grads(*order_in, hidden, pre_grad, scale, size, early, stations - early)
    pre_grad, blocks = fence((pre_grad, blocks))
    ngrad = spread(pre_grad, w_in)
    pairs, blocks, hidden, ngrad = fence((pairs, blocks, hidden, ngrad))
    keep(blocks, leaving[early:])
    sums.arrived(pairs)
    pairs = sums.step()
    ng_sib = send(ngrad[1], swap)
    branch = spread(hidden, w_out)
    ng_sib, branch = fence((ng_sib, branch))
    conv_grad, gain_local = norm_back(ngrad[0], ng_sib, white, inv, norm_gain, scale)
    conv_grad = fence(conv_grad).reshape(lat, lon, channels)
    rims = send(conv_grad[lat - RIM :], up), send(conv_grad[:RIM], down)
    taps_local = tap_sums(before, fields, after, conv_grad, scale)
    pairs, rims, taps_local, branch = fence((pairs, rims, taps_local, branch))
    sums.arrived(pairs)
    for _ in range(half - 4):
        sums.arrived(fence(sums.step()))
    pairs = sums.step()
    small = joined(jnp.concatenate([taps_local.reshape(KS * KS, channels), gain_local], axis=0), 4)
    rims, small = fence((rims, small))
    g_before, g_after = rims
    small = joined(summed(small), 8)
    fields_grad = backward_conv(g_before, conv_grad, g_after, kernel, cotangent)
    fields_grad = backward_conv(g_before, conv_grad, g_after, kernel, cotangent, fields_grad)
    br_sib = send(branch[1], swap)
    pairs, fields_grad, br_sib, small = fence((pairs, fields_grad, br_sib, small))
    sums.arrived(pairs)
    pairs = sums.step()
    small = joined(summed(small), 2)
    result = (
        fields.astype(F32) + (branch[0] + br_sib.astype(F32)).reshape(fields.shape)
    ).astype(BF16)
    small, pairs, result = fence((small, pairs, result))
    sums.arrived(pairs)
    for bit in [1 << k for k in range(4, row_devs.bit_length() - 1)] + [1]:
        small = joined(summed(small), bit)
    small = summed(small)
    kernel_grad = small[: KS * KS].reshape(KS, KS, channels)
    gain_grad = small[KS * KS]

    share = sums.total()
    rows = size // 2
    stay = lax.dynamic_slice_in_dim(share, core * rows, rows, axis=1)
    give = lax.dynamic_slice_in_dim(share, (1 - core) * rows, rows, axis=1)
    got = send(give, swap)
    final = jnp.where(
        core == 0, jnp.concatenate([stay, got], axis=2), jnp.concatenate([got, stay], axis=2)
    )
    return (result, fields_grad, final[0], final[1].T, kernel_grad, gain_grad)


def solution(mesh):
    in_specs = (
        P(("grp", "row"), None, None),
        P(None, None, "grp"),
        P("grp"),
        P(("grp", "row"), None),
        P("grp", "row"),
        P(("grp", "row"), None, None),
    )
    out_specs = (
        P(("grp", "row"), None, None),
        P(("grp", "row"), None, None),
        P(("grp", "row"), None),
        P("grp", "row"),
        P(None, None, "grp"),
        P("grp"),
    )
    return jax.shard_map(
        on_device, mesh=mesh, in_specs=in_specs, out_specs=out_specs, check_vma=False
    )
```

```python
import functools
import math

import jax
import jax.numpy as jnp
from jax import lax
from jax.experimental import pallas as pl
from jax.experimental.pallas import tpu as pltpu
from jax.sharding import PartitionSpec as P

F32 = jnp.float32
BF16 = jnp.bfloat16
KS = 7
RIM = KS // 2
LANES = 128
SUB = 8
MIB = 1024 * 1024
IN_VMEM = pl.BlockSpec(memory_space=pltpu.VMEM)


def cost(micros, nbytes=0):
    return pl.CostEstimate(flops=int(micros * 1.15e9), bytes_accessed=int(nbytes), transcendentals=0)


def params(mib):
    return pltpu.CompilerParams(vmem_limit_bytes=mib * MIB)


def whole(shape):
    return pl.BlockSpec(shape, lambda *_: (0,) * len(shape))


def fill_padded(before_ref, mid_ref, after_ref, pad_ref):
    lat, lon = mid_ref.shape[0], mid_ref.shape[1]
    for row in range(lat + 2 * RIM):
        if row < RIM:
            line = before_ref[row]
        elif row < RIM + lat:
            line = mid_ref[row - RIM]
        else:
            line = after_ref[row - RIM - lat]
        line = line.astype(F32)
        pad_ref[row, pl.ds(SUB, lon), :] = line
        pad_ref[row, pl.ds(0, SUB), :] = line[lon - SUB :]
        pad_ref[row, pl.ds(SUB + lon, SUB), :] = line[:SUB]


def conv_tile(pad_ref, weight_ref, start, lat, flip):
    totals = [None] * lat
    for b in range(KS):
        lines = [
            pad_ref[row, pl.ds(start + (SUB - RIM) + b, SUB), :] for row in range(lat + 2 * RIM)
        ]
        for a in range(KS):
            index = a * KS + b
            weight = weight_ref[KS * KS - 1 - index if flip else index]
            for row in range(lat):
                term = lines[row + a] * weight
                totals[row] = term if totals[row] is None else totals[row] + term
    return totals


def spread_weights(kern_ref, weight_ref):
    taps = kern_ref[...].astype(F32)
    for a in range(KS):
        for b in range(KS):
            weight_ref[a * KS + b] = jnp.broadcast_to(taps[a, b : b + 1], (SUB, LANES))


def conv_block(before_ref, mid_ref, after_ref, kern_ref, pad_ref, weight_ref, put, flip):
    lat, lon = mid_ref.shape[0], mid_ref.shape[1]
    fill_padded(before_ref, mid_ref, after_ref, pad_ref)
    spread_weights(kern_ref, weight_ref)

    def tile(t, carry):
        start = pl.multiple_of(t * SUB, SUB)
        for row, total in enumerate(conv_tile(pad_ref, weight_ref, start, lat, flip)):
            put(row, start, total)
        return carry

    lax.fori_loop(0, lon // SUB, tile, 0, unroll=8)


def forward_first_body(before_ref, mid_ref, after_ref, kern_ref, conv_ref, pad_ref, weight_ref):
    lon = mid_ref.shape[1]

    def put(row, start, total):
        conv_ref[0, pl.ds(pl.multiple_of(row * lon + start, SUB), SUB), :] = total

    conv_block(before_ref, mid_ref, after_ref, kern_ref, pad_ref, weight_ref, put, False)


def forward_last_body(
    before_ref, mid_ref, after_ref, kern_ref, gain_ref, first_ref, normed_ref, white_ref, inv_ref, pad_ref, weight_ref, conv_ref
):
    step = pl.program_id(0)
    lon = mid_ref.shape[1]
    done, blocks = first_ref.shape[0], conv_ref.shape[0]

    def put(row, start, total):
        conv_ref[step, pl.ds(pl.multiple_of(row * lon + start, SUB), SUB), :] = total

    conv_block(before_ref, mid_ref, after_ref, kern_ref, pad_ref, weight_ref, put, False)

    @pl.when(step == blocks - 1)
    def _():
        channels = (done + blocks) * LANES
        high = 32

        def norm(t, carry):
            at = pl.ds(pl.multiple_of(t * high, high), high)
            parts = [first_ref[j, at, :] for j in range(done)]
            parts += [conv_ref[j, at, :] for j in range(blocks)]
            mean = jnp.sum(functools.reduce(jnp.add, parts), axis=-1, keepdims=True) * (1.0 / channels)
            parts = [p - mean for p in parts]
            squares = functools.reduce(jnp.add, [p * p for p in parts])
            var = jnp.sum(squares, axis=-1, keepdims=True) * (1.0 / channels)
            inv = lax.rsqrt(var + 1e-06)
            inv_ref[at, :] = jnp.broadcast_to(inv, (high, LANES))
            for j, part in enumerate(parts):
                cols = slice(j * LANES, (j + 1) * LANES)
                white = part * inv
                white_ref[at, cols] = white
                normed_ref[at, cols] = (white * gain_ref[:, cols]).astype(BF16)
            return carry

        lax.fori_loop(0, conv_ref.shape[1] // high, norm, 0)


def conv_specs(lat, lon, offset):
    rows = lambda n: pl.BlockSpec((n, lon, LANES), lambda i: (0, 0, i + offset))
    return [rows(RIM), rows(lat), rows(RIM), pl.BlockSpec((KS, KS, LANES), lambda i: (0, 0, i + offset))]


def conv_scratch(lat, lon):
    return [
        pltpu.VMEM((lat + 2 * RIM, lon + 2 * SUB, LANES), F32),
        pltpu.VMEM((KS * KS, SUB, LANES), F32),
    ]


def forward_first(before, mid, after, kernel):
    lat, lon, channels = mid.shape
    tokens, blocks = lat * lon, channels // LANES // 2
    return pl.pallas_call(
        forward_first_body,
        grid=(blocks,),
        in_specs=conv_specs(lat, lon, 0),
        out_specs=pl.BlockSpec((1, tokens, LANES), lambda i: (i, 0, 0)),
        out_shape=jax.ShapeDtypeStruct((blocks, tokens, LANES), F32),
        scratch_shapes=conv_scratch(lat, lon),
        compiler_params=params(4),
        cost_estimate=cost(5),
        name="forward_first",
    )(before, mid, after, kernel)


def forward_last(before, mid, after, kernel, gain, first):
    lat, lon, channels = mid.shape
    tokens, done = lat * lon, first.shape[0]
    blocks = channels // LANES - done
    return pl.pallas_call(
        forward_last_body,
        grid=(blocks,),
        in_specs=conv_specs(lat, lon, done) + [whole((1, channels)), IN_VMEM],
        out_specs=[IN_VMEM] * 3,
        out_shape=[
            jax.ShapeDtypeStruct((tokens, channels), BF16),
            jax.ShapeDtypeStruct((tokens, channels), F32),
            jax.ShapeDtypeStruct((tokens, LANES), F32),
        ],
        scratch_shapes=conv_scratch(lat, lon) + [pltpu.VMEM((blocks, tokens, LANES), F32)],
        compiler_params=params(5),
        cost_estimate=cost(9),
        name="forward_last",
    )(before, mid, after, kernel, gain.reshape(1, channels), first)


def backward_body(before_ref, mid_ref, after_ref, kern_ref, cot_ref, *refs):
    out_ref, pad_ref, weight_ref, sum_ref = refs[-4:]
    lat = mid_ref.shape[0]

    def put(row, start, total):
        sum_ref[row, pl.ds(start, SUB), :] = total

    conv_block(before_ref, mid_ref, after_ref, kern_ref, pad_ref, weight_ref, put, True)
    for row in range(lat):
        out_ref[row] = (cot_ref[row].astype(F32) + sum_ref[row]).astype(BF16)


def backward_conv(before, mid, after, kernel, cot, earlier=None):
    lat, lon, channels = mid.shape
    blocks = channels // LANES // 2
    offset = 0 if earlier is None else blocks
    rows = pl.BlockSpec((lat, lon, LANES), lambda i: (0, 0, i + offset))
    more = () if earlier is None else (earlier,)
    return pl.pallas_call(
        backward_body,
        grid=(blocks,),
        in_specs=conv_specs(lat, lon, offset) + [rows] + [pl.BlockSpec(memory_space=pl.ANY)] * len(more),
        out_specs=rows,
        out_shape=jax.ShapeDtypeStruct((lat, lon, channels), BF16),
        scratch_shapes=conv_scratch(lat, lon) + [pltpu.VMEM((lat, lon, LANES), F32)],
        input_output_aliases={5: 0} if more else {},
        compiler_params=params(4),
        cost_estimate=cost(6),
        name="backward_conv",
    )(before, mid, after, kernel, cot, *more)


def tap_sums_body(scale, before_ref, mid_ref, after_ref, grad_ref, out_ref, pad_ref, wide_ref):
    lat, lon = mid_ref.shape[0], mid_ref.shape[1]
    fill_padded(before_ref, mid_ref, after_ref, pad_ref)
    for row in range(lat):
        wide_ref[row] = grad_ref[row].astype(F32)
    for b in range(KS):

        def tile(t, totals, b=b):
            start = pl.multiple_of(t * SUB, SUB)
            grads = [wide_ref[row, pl.ds(start, SUB), :] for row in range(lat)]
            lines = [
                pad_ref[row, pl.ds(start + (SUB - RIM) + b, SUB), :] for row in range(lat + 2 * RIM)
            ]
            return tuple(
                totals[a] + functools.reduce(jnp.add, [grads[row] * lines[row + a] for row in range(lat)])
                for a in range(KS)
            )

        zero = jnp.zeros((SUB, LANES), F32)
        totals = lax.fori_loop(0, lon // SUB, tile, (zero,) * KS, unroll=8)
        for a in range(KS):
            out_ref[a, b : b + 1, :] = jnp.sum(totals[a], axis=0, keepdims=True) * scale


def tap_sums(before, mid, after, grad, scale):
    lat, lon, channels = mid.shape
    tokens = lat * lon
    rows = lambda n: pl.BlockSpec((n, lon, LANES), lambda i: (0, 0, i))
    return pl.pallas_call(
        functools.partial(tap_sums_body, scale),
        grid=(channels // LANES,),
        in_specs=[rows(RIM), rows(lat), rows(RIM), rows(lat)],
        out_specs=pl.BlockSpec((KS, KS, LANES), lambda i: (0, 0, i)),
        out_shape=jax.ShapeDtypeStruct((KS, KS, channels), F32),
        scratch_shapes=[
            pltpu.VMEM((lat + 2 * RIM, lon + 2 * SUB, LANES), F32),
            pltpu.VMEM((lat, lon, LANES), F32),
        ],
        compiler_params=params(4),
        cost_estimate=cost(10),
        name="tap_sums",
    )(before, mid, after, grad)


HIGH = 256


def tiles(size):
    return [slice(t, t + HIGH) for t in range(0, size, HIGH)]


def hidden_body(n_blocks, chips_ref, n_own, n_sib, c_own, c_sib, *refs):
    shards, last = refs[: n_blocks - 1], refs[n_blocks - 1 : n_blocks + 1]
    hid_ref, grad_ref, win_ref, wout_ref, sems = refs[n_blocks + 1 :]
    size = last[0].shape[0]
    copies = []
    for j in range(n_blocks):
        at = pl.ds(pl.multiple_of(chips_ref[j] * size, size), size)
        for k, target in enumerate((win_ref, wout_ref)):
            source = shards[j].at[k] if j < n_blocks - 1 else last[k]
            copies.append(pltpu.make_async_copy(source, target.at[at, :], sems.at[2 * j + k]))
    for copy in copies:
        copy.start()
    for copy in copies:
        copy.wait()
    for half, (n_ref, c_ref) in enumerate(((n_own, c_own), (n_sib, c_sib))):

        def rows(t, carry, half=half, n_ref=n_ref, c_ref=c_ref):
            at = pl.ds(pl.multiple_of(t * HIGH, HIGH), HIGH)
            for cols in (slice(0, win_ref.shape[1]),):
                pre = jnp.dot(n_ref[at, :], win_ref[:, cols], preferred_element_type=F32)
                back = jnp.dot(c_ref[at, :], wout_ref[:, cols], preferred_element_type=F32)
                area = 0.5 * (1.0 + lax.erf(pre * (1.0 / math.sqrt(2.0))))
                dens = jnp.exp(-0.5 * pre * pre) * (1.0 / math.sqrt(2.0 * math.pi))
                hid_ref[half, at, cols] = (pre * area).astype(BF16)
                grad_ref[half, at, cols] = (back * (area + pre * dens)).astype(BF16)
            return carry

        lax.fori_loop(0, n_ref.shape[0] // HIGH, rows, 0)


def hidden_step(chips, n_own, n_sib, c_own, c_sib, shards):
    tokens, channels = n_own.shape
    width = shards[-1].shape[1]
    return pl.pallas_call(
        functools.partial(hidden_body, len(shards) - 1),
        in_specs=[pl.BlockSpec(memory_space=pltpu.SMEM)]
        + [IN_VMEM] * 4
        + [pl.BlockSpec(memory_space=pltpu.HBM)] * len(shards),
        out_specs=[IN_VMEM] * 4,
        out_shape=[
            jax.ShapeDtypeStruct((2, tokens, width), BF16),
            jax.ShapeDtypeStruct((2, tokens, width), BF16),
            jax.ShapeDtypeStruct((channels, width), BF16),
            jax.ShapeDtypeStruct((channels, width), BF16),
        ],
        scratch_shapes=[pltpu.SemaphoreType.DMA((2 * len(shards),))],
        compiler_params=params(12),
        cost_estimate=cost(17),
        name="hidden_step",
    )(chips, n_own, n_sib, c_own, c_sib, *shards)


def arrange_body(size, chips_ref, *refs):
    count = len(refs) // 2
    for source, target in zip(refs[:count], refs[count:]):
        for j in range(source.shape[1] // size):
            at = pl.ds(pl.multiple_of(chips_ref[j] * size, size), size)
            target[:, j * size : (j + 1) * size] = source[:, at]


def arrange(chips, size, values):
    if size % LANES:
        return [
            jnp.concatenate(
                [
                    lax.dynamic_slice_in_dim(v, chips[j] * size, size, axis=1)
                    for j in range(v.shape[1] // size)
                ],
                axis=1,
            )
            for v in values
        ]
    return pl.pallas_call(
        functools.partial(arrange_body, size),
        in_specs=[pl.BlockSpec(memory_space=pltpu.SMEM)] + [IN_VMEM] * len(values),
        out_specs=[IN_VMEM] * len(values),
        out_shape=[jax.ShapeDtypeStruct(v.shape, v.dtype) for v in values],
        compiler_params=params(4),
        cost_estimate=cost(2),
        name="arrange",
    )(chips, *values)


def weight_grad_body(scale, size, first, n_own, n_sib, c_own, c_sib, hid_ref, grad_ref, *outs):
    contract = (((0,), (0,)), ((), ()))
    for k, out_ref in enumerate(outs):
        at = slice((first + k) * size, (first + k + 1) * size)
        for which, (own, sib, rhs) in enumerate(((n_own, n_sib, grad_ref), (c_own, c_sib, hid_ref))):
            total = lax.dot_general(own[:, at], rhs[0], contract, preferred_element_type=F32)
            total = total + lax.dot_general(sib[:, at], rhs[1], contract, preferred_element_type=F32)
            out_ref[which] = (total * scale).astype(BF16)


def weight_grads(n_own, n_sib, c_own, c_sib, hid, grad, scale, size, first, count):
    width = hid.shape[2]
    shape = jax.ShapeDtypeStruct((2, size, width), BF16)
    return pl.pallas_call(
        functools.partial(weight_grad_body, scale, size, first),
        in_specs=[IN_VMEM] * 6,
        out_specs=[IN_VMEM] * count,
        out_shape=[shape] * count,
        compiler_params=params(12),
        cost_estimate=cost(9 * size * count / n_own.shape[1]),
        name="weight_grads",
    )(n_own, n_sib, c_own, c_sib, hid, grad)


def spread_body(lhs_ref, w_ref, own_ref, sib_ref):
    contract = (((1,), (1,)), ((), ()))
    for half, out_ref in enumerate((own_ref, sib_ref)):
        for at in tiles(lhs_ref.shape[1]):
            total = lax.dot_general(lhs_ref[half, at, :], w_ref[...], contract, preferred_element_type=F32)
            out_ref[at, :] = total.astype(out_ref.dtype)


def spread(lhs, weight):
    _, tokens, width = lhs.shape
    channels = weight.shape[0]
    return pl.pallas_call(
        spread_body,
        in_specs=[IN_VMEM] * 2,
        out_specs=[IN_VMEM] * 2,
        out_shape=[
            jax.ShapeDtypeStruct((tokens, channels), F32),
            jax.ShapeDtypeStruct((tokens, channels), BF16),
        ],
        compiler_params=params(8),
        cost_estimate=cost(4.7),
        name="spread",
    )(lhs, weight)


def norm_back_body(scale, own_ref, sib_ref, white_ref, inv_ref, gain_ref, out_ref, gsum_ref):
    channels = own_ref.shape[1]
    blocks = channels // LANES
    high = 16

    def tile(t, sums):
        at = pl.ds(pl.multiple_of(t * high, high), high)
        inv = inv_ref[at, :]
        terms, whites, new = [], [], []
        for j in range(blocks):
            cols = slice(j * LANES, (j + 1) * LANES)
            grad = own_ref[at, cols] + sib_ref[at, cols].astype(F32)
            white = white_ref[at, cols]
            new.append(sums[j] + jnp.sum((grad * white).reshape(high // SUB, SUB, LANES), axis=0))
            terms.append(grad * gain_ref[:, cols])
            whites.append(white)
        mean = jnp.sum(functools.reduce(jnp.add, terms), axis=-1, keepdims=True) * (1.0 / channels)
        cross = functools.reduce(jnp.add, [g * w for g, w in zip(terms, whites)])
        cross = jnp.sum(cross, axis=-1, keepdims=True) * (1.0 / channels)
        for j in range(blocks):
            cols = slice(j * LANES, (j + 1) * LANES)
            out_ref[at, cols] = (inv * (terms[j] - mean - whites[j] * cross)).astype(BF16)
        return tuple(new)

    zero = jnp.zeros((SUB, LANES), F32)
    sums = lax.fori_loop(0, own_ref.shape[0] // high, tile, (zero,) * blocks)
    for j in range(blocks):
        gsum_ref[:, j * LANES : (j + 1) * LANES] = jnp.sum(sums[j], axis=0, keepdims=True) * scale


def norm_back(own, sib, white, inv, gain, scale):
    tokens, channels = own.shape
    return pl.pallas_call(
        functools.partial(norm_back_body, scale),
        in_specs=[pl.BlockSpec(memory_space=pltpu.VMEM)] * 5,
        out_specs=[pl.BlockSpec(memory_space=pltpu.VMEM)] * 2,
        out_shape=[
            jax.ShapeDtypeStruct((tokens, channels), BF16),
            jax.ShapeDtypeStruct((1, channels), F32),
        ],
        compiler_params=params(4),
        cost_estimate=cost(3.5),
        name="norm_back",
    )(own, sib, white, inv, gain.reshape(1, channels))


def ring_order(stations):
    if stations == 8:
        return [0, 2, 4, 6, 7, 5, 3, 1]
    return list(range(stations))


def added(a, b):
    return (a.astype(F32) + b.astype(F32)).astype(BF16)


def on_device(fields, kernel, norm_gain, proj_in, proj_out, cotangent):
    lat, lon, channels = fields.shape
    row_devs = lax.axis_size("row")
    stations = row_devs // 2
    half = stations // 2
    scale = 1.0 / math.sqrt(lat * row_devs * lon)
    me = lax.axis_index("row")
    core, chip = me % 2, me // 2
    order = ring_order(stations)
    place = [order.index(i) for i in range(stations)]
    slots = [0] + [d for r in range(1, half) for d in (-r, r)] + [half]
    table = [[order[(place[p] + d) % stations] for d in slots] for p in range(stations)]
    chips = lax.dynamic_index_in_dim(jnp.array(table, jnp.int32), chip, 0, keepdims=False)
    leaving = [half] + [d for r in range(half - 1, 0, -1) for d in (r, -r)] + [0]
    table = [[order[(place[p] + d) % stations] for d in leaving] for p in range(stations)]
    leave = lax.dynamic_index_in_dim(jnp.array(table, jnp.int32), chip, 0, keepdims=False)

    swap = [(i, i ^ 1) for i in range(row_devs)]
    up = [(i, i + 1) for i in range(row_devs - 1)]
    down = [(i + 1, i) for i in range(row_devs - 1)]
    send = lambda value, pairs: lax.ppermute(value, "row", pairs)

    def rims_sent(value):
        last, first = value[lat - RIM :], value[:RIM]
        if stations != 8:
            return send(last, up), send(first, down)
        above = send(last, [p for p in up if p != (11, 12)])
        below = send(first, [p for p in down if p != (4, 3)])
        return above, below, send(jnp.where(core == 0, first, last), [(11, 9), (4, 6)])

    def rims_passed(rims):
        return (*rims[:2], *(send(r, [(9, 12), (6, 3)]) for r in rims[2:]))

    def rims_got(rims):
        if stations != 8:
            return rims
        above, below, far = rims
        return jnp.where(me == 12, far, above), jnp.where(me == 3, far, below)

    def ring(step):
        return [
            (order[i] * 2 + c, order[(i + step) % stations] * 2 + c)
            for i in range(stations)
            for c in range(2)
        ]

    onward, backward = ring(1), ring(-1)

    hid = proj_in.shape[1]
    mine = hid // 2
    size = channels // stations

    weights = jnp.stack([proj_in, proj_out.T])
    kept = lax.dynamic_slice_in_dim(weights, core * mine, mine, axis=2)
    given = lax.dynamic_slice_in_dim(weights, (1 - core) * mine, mine, axis=2)
    got = send(given, swap)
    shard = jnp.where(
        core == 0, jnp.concatenate([kept, got], axis=1), jnp.concatenate([got, kept], axis=1)
    )

    fence = lax.optimization_barrier

    class Gather:
        def __init__(self, part):
            self.found, self.left = [part], half
            self.pair = part, part

        def step(self):
            self.left -= 1
            on, back = self.pair
            if not self.left:
                on, back = on[0], back[1]
            self.pair = send(on, onward), send(back, backward)
            return self.pair

        def arrived(self, pair):
            self.pair = pair
            self.found += pair

    class Scatter:
        def __init__(self):
            self.d = half
            self.blocks = {}
            self.pair = None

        def step(self):
            d = self.d
            self.d = d - 1
            if d == half:
                on, back = self.blocks[d][0], self.blocks[d][1]
            else:
                on, back = self.blocks[d], self.blocks[-d]
                if d == half - 1:
                    on = jnp.stack([added(on[0], self.pair[0]), on[1]])
                    back, come, on = fence((back, self.pair[1], on))
                    back = jnp.stack([back[0], added(back[1], come)])
                else:
                    on = added(on, self.pair[0])
                    back, come, on = fence((back, self.pair[1], on))
                    back = added(back, come)
            self.pair = send(on, onward), send(back, backward)
            return self.pair

        def arrived(self, pair):
            self.pair = pair

        def total(self):
            total = self.blocks[0].astype(F32) + self.pair[0].astype(F32) + self.pair[1].astype(F32)
            return total.astype(BF16)

    def joined(value, bit):
        low = value.astype(BF16)
        return low, send(low, [(i, i ^ bit) for i in range(row_devs)])

    def summed(pair):
        return pair[0].astype(F32) + pair[1].astype(F32)

    c_own = cotangent.reshape(-1, channels)
    load, sums = Gather(shard), Scatter()
    pairs = load.step()
    rims = rims_sent(fields)
    c_sib = send(c_own, swap)
    pairs = fence(pairs)
    load.arrived(pairs)
    pairs = load.step()
    pairs, rims, c_sib = fence((pairs, rims_passed(rims), c_sib))
    load.arrived(pairs)
    for _ in range(half - 4):
        load.arrived(fence(load.step()))
    pairs = load.step()
    before, after = rims_got(rims)
    conv = forward_first(before, fields, after, kernel)
    n_own, white, inv = forward_last(before, fields, after, kernel, norm_gain, conv)
    pairs, n_own = fence((pairs, n_own))
    load.arrived(pairs)
    pairs = load.step()
    n_sib = send(n_own, swap)
    order_in = arrange(leave, size, (n_own, n_sib, c_own, c_sib))
    pairs, order_in, n_sib = fence((pairs, order_in, n_sib))
    load.arrived(pairs)
    hidden, pre_grad, w_in, w_out = hidden_step(
        chips, n_own, n_sib, c_own, c_sib, load.found
    )
    early = 3

    def keep(blocks, names):
        sums.blocks.update(zip(names, blocks))

    blocks = weight_grads(*order_in, hidden, pre_grad, scale, size, 0, early)
    blocks, hidden, pre_grad, order_in = fence((blocks, hidden, pre_grad, order_in))
    keep(blocks, leaving[:early])
    pairs = sums.step()
    blocks = weight_grads(*order_in, hidden, pre_grad, scale, size, early, stations - early)
    pre_grad, blocks = fence((pre_grad, blocks))
    ngrad = spread(pre_grad, w_in)
    pairs, blocks, hidden, ngrad = fence((pairs, blocks, hidden, ngrad))
    keep(blocks, leaving[early:])
    sums.arrived(pairs)
    pairs = sums.step()
    ng_sib = send(ngrad[1], swap)
    branch = spread(hidden, w_out)
    ng_sib, branch = fence((ng_sib, branch))
    conv_grad, gain_local = norm_back(ngrad[0], ng_sib, white, inv, norm_gain, scale)
    conv_grad = fence(conv_grad).reshape(lat, lon, channels)
    rims = send(conv_grad[lat - RIM :], up), send(conv_grad[:RIM], down)
    taps_local = tap_sums(before, fields, after, conv_grad, scale)
    pairs, rims, taps_local, branch = fence((pairs, rims, taps_local, branch))
    sums.arrived(pairs)
    for _ in range(half - 4):
        sums.arrived(fence(sums.step()))
    pairs = sums.step()
    small = joined(jnp.concatenate([taps_local.reshape(KS * KS, channels), gain_local], axis=0), 4)
    rims, small = fence((rims, small))
    g_before, g_after = rims
    small = joined(summed(small), 8)
    fields_grad = backward_conv(g_before, conv_grad, g_after, kernel, cotangent)
    fields_grad = backward_conv(g_before, conv_grad, g_after, kernel, cotangent, fields_grad)
    br_sib = send(branch[1], swap)
    pairs, fields_grad, br_sib, small = fence((pairs, fields_grad, br_sib, small))
    sums.arrived(pairs)
    pairs = sums.step()
    small = joined(summed(small), 2)
    result = (
        fields.astype(F32) + (branch[0] + br_sib.astype(F32)).reshape(fields.shape)
    ).astype(BF16)
    small, pairs, result = fence((small, pairs, result))
    sums.arrived(pairs)
    for bit in [1 << k for k in range(4, row_devs.bit_length() - 1)] + [1]:
        small = joined(summed(small), bit)
    small = summed(small)
    kernel_grad = small[: KS * KS].reshape(KS, KS, channels)
    gain_grad = small[KS * KS]

    share = sums.total()
    rows = size // 2
    stay = lax.dynamic_slice_in_dim(share, core * rows, rows, axis=1)
    give = lax.dynamic_slice_in_dim(share, (1 - core) * rows, rows, axis=1)
    got = send(give, swap)
    final = jnp.where(
        core == 0, jnp.concatenate([stay, got], axis=2), jnp.concatenate([got, stay], axis=2)
    )
    return (result, fields_grad, final[0], final[1].T, kernel_grad, gain_grad)


def solution(mesh):
    in_specs = (
        P(("grp", "row"), None, None),
        P(None, None, "grp"),
        P("grp"),
        P(("grp", "row"), None),
        P("grp", "row"),
        P(("grp", "row"), None, None),
    )
    out_specs = (
        P(("grp", "row"), None, None),
        P(("grp", "row"), None, None),
        P(("grp", "row"), None),
        P("grp", "row"),
        P(None, None, "grp"),
        P("grp"),
    )
    return jax.shard_map(
        on_device, mesh=mesh, in_specs=in_specs, out_specs=out_specs, check_vma=False
    )
```
